128 devices in a mesh: region: 64 (over y, x, z), band: 2 (over core).
Axes of the slice: x: 4, y: 4, z: 4, core: 2. Of those that a mesh axis runs over, the one named last changes fastest.
Arguments:
- emission: bfloat16 [65536, 192], P(('region', 'band')), may hold values from 0.099609375 to 10
- path_sends: int32 [128, 128, 64], P(('region', 'band')), may hold values from -1 to 511, as said below
- tile_slots: int32 [1024, 512], P(('region', 'band')), may hold values from -1 to 8191, as said below
- geometry: bfloat16 [1024, 256, 512], P(('region', 'band')), may hold values from 0.00049972534 to 0.0099487305
- absorption: bfloat16 [1024, 8, 512], P(('region', 'band')), may hold values from 0.099609375 to 1
- hour_period: int32 [24], replicated, may hold values from 0 to 2
- dwellings: int32 [262144], P(('region', 'band')), may hold values from 1 to 8
- addr_sends: int32 [128, 128, 16], P(('region', 'band')), may hold values from -1 to 2047, as said below
- addr_building: int32 [128, 128, 16], P(('region', 'band')), may hold values from 0 to 2047
Outputs:
- receiver_level: float32 [262144], P(('region', 'band'))
- building_level: float32 [262144], P(('region', 'band'))
- exposure: float32 [262144, 192], P(('region', 'band'))
The draws below stay inside these ranges and needn't reach their ends.
Inputs may be any that keep to these rules, and one draw needn't show every extreme that they name: path_sends[s, d, c] is a segment of device s or -1; the live entries of each list come first; some destination gets 64 live entries from every source. tile_slots[t, p] names a received slot s * 64 + c of the tile's device whose entry path_sends[s, d, c] is live, or is -1; live entries of a tile come first, at least 256 of them, and some tile of every device has all 512 live; a slot may feed several paths. addr_sends[s, d, c] is a receiver of device s or -1; live entries of each list come first; each receiver is named at most once over all lists; some destination gets 16 live entries from every source.
All inputs are finite; a program needn't handle non-finite values.
Results may differ from the reference program's by a relative error of at most 0.00034.
Values may be sent and summed in bfloat16 or wider, within the bound.
A program may use at most 64 MiB of HBM per device.

```python
import math
import jax
import jax.numpy as jnp
from jax import lax

BANDS = 8
HOURS = 24
SEG_DEV = 512
CAP = 64
TILE_DEV = 8
RECV_TILE = 256
PATHS_TILE = 512
CAP_ADDR = 16
BLD_DEV = 2048
SEGS = 65536
TILES = 1024
RECV_DEV = 2048
RECV = 262144
BLDS = 262144
DEVICES = 128


def path_tables(key):
    keys = jax.random.split(jax.random.fold_in(key, 11), 7)
    counts = jax.random.randint(keys[0], (DEVICES, DEVICES), 1, CAP + 1, dtype=jnp.int32)
    full_dest = jax.random.randint(keys[1], (), 0, DEVICES, dtype=jnp.int32)
    counts = jnp.where(jnp.arange(DEVICES)[None, :] == full_dest, CAP, counts)
    chosen = jax.random.randint(keys[2], (DEVICES, DEVICES, CAP), 0, SEG_DEV, dtype=jnp.int32)
    send_list = jnp.where(jnp.arange(CAP)[None, None, :] < counts[:, :, None], chosen, -1)
    source = jax.random.randint(keys[3], (DEVICES, TILE_DEV * PATHS_TILE), 0, DEVICES, dtype=jnp.int32)
    live_count = jnp.take_along_axis(counts.T, source, axis=1)
    slot_pick = jax.random.randint(keys[4], source.shape, 0, 1 << 20, dtype=jnp.int32) % live_count
    picked = (source * CAP + slot_pick).reshape(DEVICES, TILE_DEV, PATHS_TILE)
    lengths = jax.random.randint(keys[5], (DEVICES, TILE_DEV), PATHS_TILE // 2, PATHS_TILE + 1, dtype=jnp.int32)
    full_tile = jax.random.randint(keys[6], (DEVICES, 1), 0, TILE_DEV, dtype=jnp.int32)
    lengths = jnp.where(jnp.arange(TILE_DEV)[None, :] == full_tile, PATHS_TILE, lengths)
    slot_table = jnp.where(jnp.arange(PATHS_TILE)[None, None, :] < lengths[:, :, None], picked, -1)
    return (send_list.astype(jnp.int32), slot_table.reshape(DEVICES * TILE_DEV, PATHS_TILE).astype(jnp.int32))


def draw_path_sends(key, part):
    return path_tables(key)[0]


def draw_tile_slots(key, part):
    return path_tables(key)[1]


def draw_addr_sends(key, part):
    keys = jax.random.split(jax.random.fold_in(key, 23), 3)
    counts = jax.random.randint(keys[0], (DEVICES, DEVICES), 1, CAP_ADDR + 1, dtype=jnp.int32)
    full_dest = jax.random.randint(keys[1], (), 0, DEVICES, dtype=jnp.int32)
    counts = jnp.where(jnp.arange(DEVICES)[None, :] == full_dest, CAP_ADDR, counts)
    rolled = jnp.roll(counts, -full_dest, axis=1)
    starts = jnp.roll(jnp.cumsum(rolled, axis=1) - rolled, full_dest, axis=1)
    orders = jax.vmap(lambda subkey: jax.random.permutation(subkey, RECV_DEV))(jax.random.split(keys[2], DEVICES))
    position = starts[:, :, None] + jnp.arange(CAP_ADDR)[None, None, :]
    is_live = (jnp.arange(CAP_ADDR)[None, None, :] < counts[:, :, None]) & (position < RECV_DEV)
    named = jnp.take_along_axis(orders, jnp.minimum(position, RECV_DEV - 1).reshape(DEVICES, -1), axis=1)
    named = named.reshape(DEVICES, DEVICES, CAP_ADDR)
    return jnp.where(is_live, named, -1).astype(jnp.int32)


def touch_ends(drawn, own_key, low, high):
    extent = drawn.shape
    index_at = [jax.random.randint(jax.random.fold_in(own_key, axis), (), 0, extent[axis]) for axis in range(len(extent))]
    drawn = drawn.at[tuple(index_at)].set(low)
    longest = extent.index(max(extent))
    index_at[longest] = (index_at[longest] + 1) % extent[longest]
    return drawn.at[tuple(index_at)].set(high)


def block_scale(rng, extent, cuts, low, top_value):
    level, own = 1.0, jax.random.fold_in(rng, 6)
    for dim, blocks in cuts:
        heights = jnp.exp(jax.random.uniform(jax.random.fold_in(own, dim), (blocks,), jnp.float32, low / len(cuts), top_value / len(cuts)))
        level = level * jnp.repeat(heights, extent[dim] // blocks).reshape([-1 if axis == dim else 1 for axis in range(len(extent))])
    return level


def setup_inputs(seed: int = 0) -> dict:
    splits = jax.random.split(jax.random.key(seed), 10)
    emission = jnp.clip(jnp.exp(math.log(10.0) - 4.609084 * jax.random.uniform(splits[0], (SEGS, BANDS * HOURS), jnp.float32) ** block_scale(splits[0], (SEGS, BANDS * HOURS), ((0, 128),), -0.2, 0.2)), 0.099609375, 10.0).astype(jnp.bfloat16)
    path_sends = draw_path_sends(jax.random.fold_in(splits[9], 71), 0)
    tile_slots = draw_tile_slots(jax.random.fold_in(splits[9], 71), 0)
    geometry = jnp.clip(jnp.exp(math.log(0.0099487305) - 2.9911416 * jax.random.uniform(splits[3], (TILES, RECV_TILE, PATHS_TILE), jnp.float32) ** block_scale(splits[3], (TILES, RECV_TILE, PATHS_TILE), ((0, 128),), -0.2, 0.2)), 0.00049972534, 0.0099487305).astype(jnp.bfloat16)
    absorption = jnp.clip(jnp.exp(math.log(1.0) - 2.306499 * jax.random.uniform(splits[4], (TILES, BANDS, PATHS_TILE), jnp.float32) ** block_scale(splits[4], (TILES, BANDS, PATHS_TILE), ((0, 128),), -0.2, 0.2)), 0.099609375, 1.0).astype(jnp.bfloat16)
    hour_period = touch_ends(jax.random.randint(splits[5], (HOURS,), 0, 3), jax.random.fold_in(splits[5], 1), 0, 2).astype(jnp.int32)
    dwellings = touch_ends(jax.random.randint(splits[6], (RECV,), 1, 9), jax.random.fold_in(splits[6], 1), 1, 8).astype(jnp.int32)
    addr_sends = draw_addr_sends(jax.random.fold_in(splits[9], 71), 0)
    addr_building = touch_ends(jax.random.randint(splits[8], (DEVICES, DEVICES, CAP_ADDR), 0, BLD_DEV), jax.random.fold_in(splits[8], 1), 0, BLD_DEV - 1).astype(jnp.int32)
    return {"emission": emission, "path_sends": path_sends, "tile_slots": tile_slots, "geometry": geometry, "absorption": absorption, "hour_period": hour_period, "dwellings": dwellings, "addr_sends": addr_sends, "addr_building": addr_building}


A_WEIGHTING_DB = [-26.2, -16.1, -8.6, -3.2, 0.0, 1.2, 1.0, -1.1]


def hour_weights(hour_period):
    a_weight = jnp.power(10.0, jnp.array(A_WEIGHTING_DB, jnp.float32) / 10.0)
    period_gain = jnp.array([1.0, 10.0 ** 0.5, 10.0], jnp.float32)
    matches = hour_period[:, None] == jnp.arange(3, dtype=jnp.int32)[None, :]
    per_hour = jnp.sum(jnp.where(matches, period_gain[None, :], jnp.float32(0.0)), axis=1)
    return (a_weight[:, None] * per_hour[None, :] / HOURS).reshape(-1)


def device_levels(emission, weights, items):
    send_column, slot_table, geometry, absorption = items
    row_index = jnp.arange(DEVICES, dtype=jnp.int32)[:, None] * SEG_DEV + jnp.maximum(send_column, 0)
    arrived = jnp.where(send_column[:, :, None] >= 0, emission[row_index], jnp.zeros((), jnp.bfloat16))
    arrived = arrived.reshape(DEVICES * CAP, BANDS * HOURS)
    gathered = jnp.where(slot_table[:, :, None] >= 0, arrived[jnp.maximum(slot_table, 0)], jnp.zeros((), jnp.bfloat16))
    factor = jnp.repeat(jnp.swapaxes(absorption, 1, 2), HOURS, axis=2)
    mixed_rows = (factor.astype(jnp.float32) * gathered.astype(jnp.float32)).astype(jnp.bfloat16)
    exposure = jnp.einsum("trp,tpc->trc", geometry.astype(jnp.float32), mixed_rows.astype(jnp.float32))
    flat_rows = exposure.reshape(-1, BANDS * HOURS)
    energy = jnp.dot(flat_rows, weights, precision=lax.Precision.HIGHEST)
    return jnp.log10(energy), flat_rows


def reference(emission, path_sends, tile_slots, geometry, absorption, hour_period, dwellings, addr_sends, addr_building):
    weights = hour_weights(hour_period)
    items = (jnp.swapaxes(path_sends, 0, 1),
             tile_slots.reshape(DEVICES, TILE_DEV, PATHS_TILE),
             geometry.reshape(DEVICES, TILE_DEV, RECV_TILE, PATHS_TILE),
             absorption.reshape(DEVICES, TILE_DEV, BANDS, PATHS_TILE))
    levels, exposure = lax.map(lambda piece: device_levels(emission, weights, piece), items)
    safe_index = jnp.maximum(addr_sends, 0).reshape(DEVICES, -1)
    is_live = addr_sends >= 0
    level_at = jnp.take_along_axis(levels, safe_index, axis=1).reshape(addr_sends.shape)
    dwell_all = dwellings.reshape(DEVICES, RECV_DEV).astype(jnp.float32)
    dwell_at = jnp.take_along_axis(dwell_all, safe_index, axis=1).reshape(addr_sends.shape)
    dwelt = jnp.where(is_live, dwell_at, jnp.float32(0.0))
    weighted = jnp.where(is_live, dwell_at * level_at, jnp.float32(0.0))
    dwelt = jnp.swapaxes(dwelt, 0, 1)
    weighted = jnp.swapaxes(weighted, 0, 1)
    segment_ids = jnp.arange(DEVICES, dtype=jnp.int32)[:, None, None] * BLD_DEV + addr_building
    numer = jax.ops.segment_sum(weighted.reshape(-1), segment_ids.reshape(-1), num_segments=BLDS)
    denom = jax.ops.segment_sum(dwelt.reshape(-1), segment_ids.reshape(-1), num_segments=BLDS)
    building_level = numer / jnp.maximum(denom, jnp.float32(1.0))
    return levels.reshape(-1), building_level, exposure.reshape(-1, BANDS * HOURS)
```

```python
import math

import jax
import jax.numpy as jnp
from jax import lax
from jax.experimental import pallas as pl
from jax.experimental.pallas import tpu as pltpu
from jax.sharding import PartitionSpec as P

BANDS = 8
HOURS = 24
WIDTH = BANDS * HOURS
SEG_DEV = 512
CAP = 64
TILE_DEV = 8
RECV_TILE = 256
PATHS_TILE = 512
CAP_ADDR = 16
DEVICES = 128
PATHS = TILE_DEV * PATHS_TILE
BLOCK = 96
MIX, UNMIX = 45, 37
GROUP = 16
PICK = 4
A_WEIGHTING_DB = (-26.2, -16.1, -8.6, -3.2, 0.0, 1.2, 1.0, -1.1)
MESH = pl.DeviceIdType.MESH
BF16, F32, I32 = jnp.bfloat16, jnp.float32, jnp.int32


def my_place():
    region, core = lax.axis_index("region"), lax.axis_index("band")
    return region // 16, (region // 4) % 4, region % 4, core


def peer(step):
    y, x, z, core = my_place()
    shift = (step * MIX) % DEVICES
    region = ((y + shift // 32) % 4) * 16 + ((x + (shift // 8) % 4) % 4) * 4 + (z + (shift // 2) % 4) % 4
    return region, (core + shift) % 2


def step_of_source(source):
    y, x, z, core = my_place()
    dy = (y + 4 - source // 32) % 4
    dx = (x + 4 - (source // 8) % 4) % 4
    dz = (z + 4 - (source // 2) % 4) % 4
    dc = (core + 2 - source % 2) % 2
    return ((dy * 32 + dx * 8 + dz * 2 + dc) * UNMIX) % DEVICES


def split3(value):
    high = value.astype(BF16)
    rest = value - high.astype(F32)
    mid = rest.astype(BF16)
    return high, mid, (rest - mid.astype(F32)).astype(BF16)


def kernel(
    em_ref, ps_ref, slot_ref, geo_hbm, abs_ref, hour_ref, dwell_ref, addr_ref, bld_ref,
    level_ref, build_ref, expo_ref,
    rows, outb, recv, rhs, acc, hi_ref, lo_ref, geo, weight, msg_out, msg_in,
    geo_sem, self_sem, send_sem, recv_sem, msend_sem, mrecv_sem,
):
    region, core = lax.axis_index("region"), lax.axis_index("band")
    me = region * 2 + core
    geo_copy = pltpu.make_async_copy(geo_hbm, geo, geo_sem)
    geo_copy.start()
    barrier = pltpu.get_barrier_semaphore()

    def greet(step, carry):
        pl.semaphore_signal(barrier, inc=1, device_id=peer(step), device_id_type=MESH)
        return carry

    lax.fori_loop(1, DEVICES, greet, 0)

    em = em_ref[...].astype(F32)
    rows[...] = jnp.concatenate([em, em[128:192]], axis=0).T.astype(BF16)
    lists = ps_ref[...].astype(F32)
    low_lanes = lax.broadcasted_iota(I32, (32, 128), 1) < 64

    def pick(group):
        columns = []
        for u in range(PICK):
            to_region, to_core = peer(group * PICK + u)
            dest = to_region * 2 + to_core
            hit = lax.broadcasted_iota(I32, (CAP, DEVICES), 1) == dest
            columns.append(jnp.sum(jnp.where(hit, lists, 0.0), axis=1, keepdims=True))
        column = jnp.concatenate(columns, axis=0)
        lane = lax.broadcasted_iota(I32, (PICK * CAP, SEG_DEV), 1).astype(F32)
        table = jnp.where(lane == column, 1.0, 0.0).astype(BF16)
        picked = jnp.dot(table, rows[...], preferred_element_type=F32).astype(BF16)
        for u in range(PICK):
            step = group * PICK + u
            block = picked[u * CAP : (u + 1) * CAP]
            outb[step, 0:64, :] = block[:, 0:128]
            outb[step, 64:96, :] = jnp.where(low_lanes, block[0:32, 128:256], block[32:64, 128:256])

    def send(step):
        pltpu.make_async_remote_copy(
            src_ref=outb.at[step], dst_ref=recv.at[step], send_sem=send_sem, recv_sem=recv_sem.at[step // GROUP],
            device_id=peer(step), device_id_type=MESH,
        ).start()

    pick(0)
    pl.semaphore_wait(barrier, DEVICES - 1)
    own_copy = pltpu.make_async_copy(outb.at[0], recv.at[0], self_sem)
    own_copy.start()
    for u in range(1, PICK):
        send(u)

    def pick_and_send(group, carry):
        pick(group)
        for u in range(PICK):
            send(group * PICK + u)
        return carry

    lax.fori_loop(1, DEVICES // PICK, pick_and_send, 0)

    slots = slot_ref[...]
    safe = jnp.maximum(slots, 0)
    place = step_of_source(safe // CAP) * CAP + safe % CAP
    label = jnp.where(slots >= 0, place, -1)
    high = (label // 256).astype(F32)
    low = (label % 256).astype(F32)
    high = jnp.where(slots >= 0, high, -1.0)
    for t in range(TILE_DEV):
        for q in range(PATHS_TILE // 128):
            at = pl.ds(t * PATHS_TILE + q * 128, 128)
            cols = slice(q * 128, (q + 1) * 128)
            hi_ref[at, :] = jnp.broadcast_to(high[t : t + 1, cols], (128, 128)).T.astype(BF16)
            lo_ref[at, :] = jnp.broadcast_to(low[t : t + 1, cols], (128, 128)).T.astype(BF16)

    r = lax.broadcasted_iota(I32, (WIDTH, 128), 0)
    scale = jnp.zeros((WIDTH, 128), F32)
    for b in range(BANDS):
        scale = jnp.where(r // HOURS == b, jnp.float32(10.0 ** (A_WEIGHTING_DB[b] / 10.0)), scale)
    gain = jnp.zeros((WIDTH, 128), F32)
    for h in range(HOURS):
        period = hour_ref[h]
        g = jnp.where(period == 0, 1.0, jnp.where(period == 1, jnp.float32(10.0**0.5), jnp.where(period == 2, 10.0, 0.0)))
        gain = jnp.where(r % HOURS == h, g.astype(F32), gain)
    weight[...] = scale * gain / HOURS

    acc[...] = jnp.zeros_like(acc)
    ROWS = 1024

    def gather(group, carry):
        blocks = recv[pl.ds(group * GROUP, GROUP)]
        main = blocks[:, 0:64, :].reshape(GROUP * CAP, 128)
        side = blocks[:, 64:96, :]
        rhs[:, 0:128] = main
        rhs[:, 128:256] = jnp.concatenate([side, side], axis=1).reshape(GROUP * CAP, 128)

        def some_paths(i, inner):
            at = pl.ds(pl.multiple_of(i * ROWS, ROWS), ROWS)
            lo, hi = lo_ref[at, :], hi_ref[at, :]
            parts = []
            for u in range(GROUP * CAP // 256):
                here = (group * (GROUP * CAP // 256) + u).astype(F32).astype(BF16)
                own = jnp.where(hi == here, lo, BF16(-1))
                for half in range(2):
                    lane = (lax.broadcasted_iota(I32, (ROWS, 128), 1) + half * 128).astype(F32).astype(BF16)
                    parts.append(jnp.where(own == lane, BF16(1), BF16(0)))
            table = jnp.concatenate(parts, axis=1)
            acc[at, :] = acc[at, :] + jnp.dot(table, rhs[...], preferred_element_type=F32)
            return inner

        lax.fori_loop(0, PATHS // ROWS, some_paths, 0)
        return carry

    def arrived(group):
        ref = recv.at[pl.ds(group * GROUP, GROUP)]
        return pltpu.make_async_copy(ref, ref, recv_sem.at[group])

    own_copy.wait()
    first = recv.at[pl.ds(1, GROUP - 1)]
    pltpu.make_async_copy(first, first, recv_sem.at[0]).wait()
    gather(jnp.int32(0), 0)

    def wait_and_gather(group, carry):
        arrived(group).wait()
        return gather(group, carry)

    lax.fori_loop(1, DEVICES // GROUP, wait_and_gather, 0)
    geo_copy.wait()

    def tile(t, carry):
        table = acc[pl.ds(pl.multiple_of(t * PATHS_TILE, PATHS_TILE), PATHS_TILE), :].T
        first_half = slot_ref[pl.ds(t, 1), :] % CAP < 32
        tail = jnp.where(first_half, table[128:192], table[192:256])
        gathered = jnp.concatenate([table[0:128], tail], axis=0)
        damp = abs_ref[t].astype(F32)
        factor = jnp.concatenate(
            [jnp.broadcast_to(damp[b : b + 1], (HOURS, PATHS_TILE)) for b in range(BANDS)], axis=0
        )
        mixed = (factor * gathered).astype(BF16)
        exposure = lax.dot_general(mixed, geo[t], (((1,), (1,)), ((), ())), preferred_element_type=F32)
        expo_ref[:, pl.ds(pl.multiple_of(t * RECV_TILE, RECV_TILE), RECV_TILE)] = exposure
        for half in range(2):
            energy = jnp.sum(exposure[:, half * 128 : (half + 1) * 128] * weight[...], axis=0, keepdims=True)
            level_ref[pl.ds(2 * t + half, 1), :] = jnp.log(energy) * jnp.float32(1.0 / math.log(10.0))
        return carry

    lax.fori_loop(0, TILE_DEV, tile, 0)

    dwell = dwell_ref[...].astype(F32)
    table = jnp.concatenate([*split3(dwell * level_ref[...]), dwell.astype(BF16)], axis=0)
    addr = addr_ref[...]
    addr_high, addr_low = jnp.maximum(addr, 0) // 128, jnp.where(addr >= 0, addr % 128, -1)
    sub = lax.broadcasted_iota(I32, (128, 128), 0)
    weighted, dwelt = [], []
    for c in range(CAP_ADDR):
        hot = jnp.where(sub == addr_low[c : c + 1], 1.0, 0.0).astype(BF16)
        found = jnp.dot(table, hot, preferred_element_type=F32)
        level_rows = found[0:16] + found[16:32] + found[32:48]
        mine = lax.broadcasted_iota(I32, (16, 128), 0) == addr_high[c : c + 1]
        weighted.append(jnp.sum(jnp.where(mine, level_rows, 0.0), axis=0, keepdims=True))
        dwelt.append(jnp.sum(jnp.where(mine, found[48:64], 0.0), axis=0, keepdims=True))
    message = jnp.concatenate(weighted + dwelt + [jnp.zeros((96, 128), F32)], axis=0).T
    msg_out[:, 0, :] = message
    msg_in[pl.ds(me, 1)] = msg_out[pl.ds(me, 1)]

    def post(step, carry):
        to_region, to_core = peer(step)
        pltpu.make_async_remote_copy(
            src_ref=msg_out.at[to_region * 2 + to_core], dst_ref=msg_in.at[me], send_sem=msend_sem, recv_sem=mrecv_sem,
            device_id=(to_region, to_core), device_id_type=MESH,
        ).start()
        return carry

    lax.fori_loop(1, DEVICES, post, 0)
    all_in = msg_in.at[pl.ds(0, DEVICES - 1)]
    pltpu.make_async_copy(all_in, all_in, mrecv_sem).wait()

    got = msg_in[:, 0, :].T
    bld = bld_ref[...]
    bld_high, bld_low = bld // 128, bld % 128
    lhs, hots = [], []
    for c in range(CAP_ADDR):
        mine = lax.broadcasted_iota(I32, (16, 128), 0) == bld_high[c : c + 1]
        spread = jnp.where(mine, got[c : c + 1], 0.0)
        count = jnp.where(mine, got[16 + c : 17 + c], 0.0)
        lhs.append(jnp.concatenate([*split3(spread), count.astype(BF16)], axis=0))
        hots.append(jnp.where(sub == bld_low[c : c + 1], 1.0, 0.0).astype(BF16))
    sums = lax.dot_general(
        jnp.concatenate(lhs, axis=1), jnp.concatenate(hots, axis=1), (((1,), (1,)), ((), ())), preferred_element_type=F32
    )
    build_ref[...] = (sums[0:16] + sums[16:32] + sums[32:48]) / jnp.maximum(sums[48:64], 1.0)

    all_out = outb.at[pl.ds(0, DEVICES - 1)]
    pltpu.make_async_copy(all_out, all_out, send_sem).wait()
    all_mail = msg_out.at[pl.ds(0, DEVICES - 1)]
    pltpu.make_async_copy(all_mail, all_mail, msend_sem).wait()


def local(emission, path_sends, tile_slots, geometry, absorption, hour_period, dwellings, addr_sends, addr_building):
    vmem = pl.BlockSpec(memory_space=pltpu.VMEM)
    level, building, exposure = pl.pallas_call(
        kernel,
        out_shape=(
            jax.ShapeDtypeStruct((16, 128), F32),
            jax.ShapeDtypeStruct((16, 128), F32),
            jax.ShapeDtypeStruct((WIDTH, TILE_DEV * RECV_TILE), F32),
        ),
        in_specs=[vmem, vmem, vmem, pl.BlockSpec(memory_space=pl.ANY), vmem, pl.BlockSpec(memory_space=pltpu.SMEM), vmem, vmem, vmem],
        out_specs=(vmem, vmem, vmem),
        scratch_shapes=[
            pltpu.VMEM((SEG_DEV, 256), BF16),
            pltpu.VMEM((DEVICES, BLOCK, 128), BF16),
            pltpu.VMEM((DEVICES, BLOCK, 128), BF16),
            pltpu.VMEM((GROUP * CAP, 256), BF16),
            pltpu.VMEM((PATHS, 256), F32),
            pltpu.VMEM((PATHS, 128), BF16),
            pltpu.VMEM((PATHS, 128), BF16),
            pltpu.VMEM((TILE_DEV, RECV_TILE, PATHS_TILE), BF16),
            pltpu.VMEM((WIDTH, 128), F32),
            pltpu.VMEM((DEVICES, 1, 128), F32),
            pltpu.VMEM((DEVICES, 1, 128), F32),
            pltpu.SemaphoreType.DMA,
            pltpu.SemaphoreType.DMA,
            pltpu.SemaphoreType.DMA,
            pltpu.SemaphoreType.DMA((DEVICES // GROUP,)),
            pltpu.SemaphoreType.DMA,
            pltpu.SemaphoreType.DMA,
        ],
        compiler_params=pltpu.CompilerParams(collective_id=0, has_side_effects=True, vmem_limit_bytes=56 * 2**20),
        name="noise_map",
    )(
        emission.T,
        path_sends[0].T,
        tile_slots,
        geometry,
        absorption,
        hour_period,
        dwellings.reshape(16, 128),
        addr_sends[0].T,
        addr_building[0].T,
    )
    return level.reshape(-1), building.reshape(-1), exposure.T


def solution(mesh):
    both = ("region", "band")
    in_specs = (P(both, None), P(both, None, None), P(both, None), P(both, None, None), P(both, None, None), P(), P(both), P(both, None, None), P(both, None, None))
    out_specs = (P(both), P(both), P(both, None))
    return jax.shard_map(local, mesh=mesh, in_specs=in_specs, out_specs=out_specs, check_vma=False)
```

```python
import math

import jax
import jax.numpy as jnp
from jax import lax
from jax.experimental import pallas as pl
from jax.experimental.pallas import tpu as pltpu
from jax.sharding import PartitionSpec as P

BANDS = 8
HOURS = 24
WIDTH = BANDS * HOURS
SEG_DEV = 512
CAP = 64
TILE_DEV = 8
RECV_TILE = 256
PATHS_TILE = 512
CAP_ADDR = 16
DEVICES = 128
PATHS = TILE_DEV * PATHS_TILE
BLOCK = 96
MIX, UNMIX = 45, 37
GROUP = 16
PICK = 4
A_WEIGHTING_DB = (-26.2, -16.1, -8.6, -3.2, 0.0, 1.2, 1.0, -1.1)
MESH = pl.DeviceIdType.MESH
BF16, F32, I32 = jnp.bfloat16, jnp.float32, jnp.int32


def my_place():
    region, core = lax.axis_index("region"), lax.axis_index("band")
    return region // 16, (region // 4) % 4, region % 4, core


def peer(step):
    y, x, z, core = my_place()
    shift = (step * MIX) % DEVICES
    region = ((y + shift // 32) % 4) * 16 + ((x + (shift // 8) % 4) % 4) * 4 + (z + (shift // 2) % 4) % 4
    return region, (core + shift) % 2


def step_of_source(source):
    y, x, z, core = my_place()
    dy = (y + 4 - source // 32) % 4
    dx = (x + 4 - (source // 8) % 4) % 4
    dz = (z + 4 - (source // 2) % 4) % 4
    dc = (core + 2 - source % 2) % 2
    return ((dy * 32 + dx * 8 + dz * 2 + dc) * UNMIX) % DEVICES


def split3(value):
    high = value.astype(BF16)
    rest = value - high.astype(F32)
    mid = rest.astype(BF16)
    return high, mid, (rest - mid.astype(F32)).astype(BF16)


def kernel(
    em_ref, ps_ref, slot_ref, geo_hbm, abs_ref, hour_ref, dwell_ref, addr_ref,
    level_ref, msg_ref, expo_ref,
    rows, outb, recv, rhs, acc, hi_ref, lo_ref, geo, weight, first, second, hots, out_a, in_a, out_b, in_b,
    geo_sem, self_sem, send_sem, recv_sem, msend_sem, nsend_sem, mrecv_sem,
):
    core = lax.axis_index("band")
    geo_copy = pltpu.make_async_copy(geo_hbm, geo, geo_sem)
    geo_copy.start()
    barrier = pltpu.get_barrier_semaphore()

    def greet(step, carry):
        pl.semaphore_signal(barrier, inc=1, device_id=peer(step), device_id_type=MESH)
        return carry

    lax.fori_loop(1, DEVICES, greet, 0)

    em = em_ref[...].astype(F32)
    rows[...] = jnp.concatenate([em, em[128:192]], axis=0).T.astype(BF16)
    lists = ps_ref[...].astype(F32)
    low_lanes = lax.broadcasted_iota(I32, (32, 128), 1) < 64

    def pick(group):
        columns = []
        for u in range(PICK):
            to_region, to_core = peer(group * PICK + u)
            dest = to_region * 2 + to_core
            hit = lax.broadcasted_iota(I32, (CAP, DEVICES), 1) == dest
            columns.append(jnp.sum(jnp.where(hit, lists, 0.0), axis=1, keepdims=True))
        column = jnp.concatenate(columns, axis=0)
        lane = lax.broadcasted_iota(I32, (PICK * CAP, SEG_DEV), 1).astype(F32)
        table = jnp.where(lane == column, 1.0, 0.0).astype(BF16)
        picked = jnp.dot(table, rows[...], preferred_element_type=F32).astype(BF16)
        for u in range(PICK):
            step = group * PICK + u
            block = picked[u * CAP : (u + 1) * CAP]
            outb[step, 0:64, :] = block[:, 0:128]
            outb[step, 64:96, :] = jnp.where(low_lanes, block[0:32, 128:256], block[32:64, 128:256])

    def send(step):
        pltpu.make_async_remote_copy(
            src_ref=outb.at[step], dst_ref=recv.at[step], send_sem=send_sem, recv_sem=recv_sem.at[step // GROUP],
            device_id=peer(step), device_id_type=MESH,
        ).start()

    pick(0)
    pl.semaphore_wait(barrier, DEVICES - 1)
    own_copy = pltpu.make_async_copy(outb.at[0], recv.at[0], self_sem)
    own_copy.start()
    for u in range(1, PICK):
        send(u)

    def pick_and_send(group, carry):
        pick(group)
        for u in range(PICK):
            send(group * PICK + u)
        return carry

    lax.fori_loop(1, DEVICES // PICK, pick_and_send, 0)

    slots = slot_ref[...]
    safe = jnp.maximum(slots, 0)
    place = step_of_source(safe // CAP) * CAP + safe % CAP
    label = jnp.where(slots >= 0, place, -1)
    high = (label // 256).astype(F32)
    low = (label % 256).astype(F32)
    high = jnp.where(slots >= 0, high, -1.0)
    for t in range(TILE_DEV):
        for q in range(PATHS_TILE // 128):
            at = pl.ds(t * PATHS_TILE + q * 128, 128)
            cols = slice(q * 128, (q + 1) * 128)
            hi_ref[at, :] = jnp.broadcast_to(high[t : t + 1, cols], (128, 128)).T.astype(BF16)
            lo_ref[at, :] = jnp.broadcast_to(low[t : t + 1, cols], (128, 128)).T.astype(BF16)

    r = lax.broadcasted_iota(I32, (WIDTH, 128), 0)
    scale = jnp.zeros((WIDTH, 128), F32)
    for b in range(BANDS):
        scale = jnp.where(r // HOURS == b, jnp.float32(10.0 ** (A_WEIGHTING_DB[b] / 10.0)), scale)
    gain = jnp.zeros((WIDTH, 128), F32)
    for h in range(HOURS):
        period = hour_ref[h]
        g = jnp.where(period == 0, 1.0, jnp.where(period == 1, jnp.float32(10.0**0.5), jnp.where(period == 2, 10.0, 0.0)))
        gain = jnp.where(r % HOURS == h, g.astype(F32), gain)
    weight[...] = scale * gain / HOURS

    addr = permuted(
        addr_ref[...], lambda k: pl.ds(k // 2 * 32 + k % 2, 16, stride=2), lambda k: pl.ds(k * 16, 16), first, second
    )
    addr_high = jnp.maximum(addr, 0) // 128
    addr_low = jnp.where(addr >= 0, addr % 128, -1)
    sub = lax.broadcasted_iota(I32, (128, 128), 0)
    for c in range(CAP_ADDR):
        hots[:, c * 128 : (c + 1) * 128] = jnp.where(sub == addr_low[c : c + 1], 1.0, 0.0).astype(BF16)

    acc[...] = jnp.zeros_like(acc)
    ROWS = 1024

    def gather(group, carry):
        blocks = recv[pl.ds(group * GROUP, GROUP)]
        main = blocks[:, 0:64, :].reshape(GROUP * CAP, 128)
        side = blocks[:, 64:96, :]
        rhs[:, 0:128] = main
        rhs[:, 128:256] = jnp.concatenate([side, side], axis=1).reshape(GROUP * CAP, 128)

        def some_paths(i, inner):
            at = pl.ds(pl.multiple_of(i * ROWS, ROWS), ROWS)
            lo, hi = lo_ref[at, :], hi_ref[at, :]
            parts = []
            for u in range(GROUP * CAP // 256):
                here = (group * (GROUP * CAP // 256) + u).astype(F32).astype(BF16)
                own = jnp.where(hi == here, lo, BF16(-1))
                for half in range(2):
                    lane = (lax.broadcasted_iota(I32, (ROWS, 128), 1) + half * 128).astype(F32).astype(BF16)
                    parts.append(jnp.where(own == lane, BF16(1), BF16(0)))
            table = jnp.concatenate(parts, axis=1)
            acc[at, :] = acc[at, :] + jnp.dot(table, rhs[...], preferred_element_type=F32)
            return inner

        lax.fori_loop(0, PATHS // ROWS, some_paths, 0)
        return carry

    def arrived(group):
        ref = recv.at[pl.ds(group * GROUP, GROUP)]
        return pltpu.make_async_copy(ref, ref, recv_sem.at[group])

    own_copy.wait()
    first = recv.at[pl.ds(1, GROUP - 1)]
    pltpu.make_async_copy(first, first, recv_sem.at[0]).wait()
    gather(jnp.int32(0), 0)

    def wait_and_gather(group, carry):
        arrived(group).wait()
        return gather(group, carry)

    lax.fori_loop(1, DEVICES // GROUP, wait_and_gather, 0)
    geo_copy.wait()

    def tile(t, carry):
        table = acc[pl.ds(pl.multiple_of(t * PATHS_TILE, PATHS_TILE), PATHS_TILE), :].T
        first_half = slot_ref[pl.ds(t, 1), :] % CAP < 32
        tail = jnp.where(first_half, table[128:192], table[192:256])
        gathered = jnp.concatenate([table[0:128], tail], axis=0)
        damp = abs_ref[t].astype(F32)
        factor = jnp.concatenate(
            [jnp.broadcast_to(damp[b : b + 1], (HOURS, PATHS_TILE)) for b in range(BANDS)], axis=0
        )
        mixed = (factor * gathered).astype(BF16)
        exposure = lax.dot_general(mixed, geo[t], (((1,), (1,)), ((), ())), preferred_element_type=F32)
        expo_ref[:, pl.ds(pl.multiple_of(t * RECV_TILE, RECV_TILE), RECV_TILE)] = exposure
        for half in range(2):
            energy = jnp.sum(exposure[:, half * 128 : (half + 1) * 128] * weight[...], axis=0, keepdims=True)
            level_ref[pl.ds(2 * t + half, 1), :] = jnp.log(energy) * jnp.float32(1.0 / math.log(10.0))
        return carry

    lax.fori_loop(0, TILE_DEV, tile, 0)

    dwell = dwell_ref[...].astype(F32)
    table = jnp.concatenate([*split3(dwell * level_ref[...]), dwell.astype(BF16)], axis=0)
    found = jnp.dot(table, hots[...], preferred_element_type=F32)
    level_rows = found[0:16] + found[16:32] + found[32:48]
    weighted, dwelt = [], []
    for c in range(CAP_ADDR):
        lanes = slice(c * 128, (c + 1) * 128)
        mine = lax.broadcasted_iota(I32, (16, 128), 0) == addr_high[c : c + 1]
        weighted.append(jnp.sum(jnp.where(mine, level_rows[:, lanes], 0.0), axis=0, keepdims=True))
        dwelt.append(jnp.sum(jnp.where(mine, found[48:64, lanes], 0.0), axis=0, keepdims=True))
    out_a[...] = jnp.concatenate(weighted + dwelt + [jnp.zeros((96, 128), F32)], axis=0).T.reshape(8, 16, 128)
    y, x, z, _ = my_place()
    mine_a, mine_b = y * 2 + core, x * 4 + z
    in_a[mine_a] = out_a[mine_a]
    for k in range(1, 8):
        to_y, to_core = (y + k // 2) % 4, (core + k % 2) % 2
        pltpu.make_async_remote_copy(
            src_ref=out_a.at[to_y * 2 + to_core], dst_ref=in_a.at[mine_a], send_sem=msend_sem, recv_sem=mrecv_sem.at[0],
            device_id=(to_y * 16 + mine_b, to_core), device_id_type=MESH,
        ).start()
    seven = in_a.at[pl.ds(0, 7)]
    pltpu.make_async_copy(seven, seven, mrecv_sem.at[0]).wait()
    for k in range(8):
        out_b[:, k, :] = in_a[k]
    in_b[mine_b] = out_b[mine_b]
    for k in range(1, 16):
        to = ((x + k // 4) % 4) * 4 + (z + k % 4) % 4
        pltpu.make_async_remote_copy(
            src_ref=out_b.at[to], dst_ref=in_b.at[mine_b], send_sem=nsend_sem, recv_sem=mrecv_sem.at[1],
            device_id=(y * 16 + to, core), device_id_type=MESH,
        ).start()
    fifteen = in_b.at[pl.ds(0, 15)]
    pltpu.make_async_copy(fifteen, fifteen, mrecv_sem.at[1]).wait()
    msg_ref[...] = in_b[...]

    all_out = outb.at[pl.ds(0, DEVICES - 1)]
    pltpu.make_async_copy(all_out, all_out, send_sem).wait()
    sent_a, sent_b = out_a.at[pl.ds(0, 7)], out_b.at[pl.ds(0, 15)]
    pltpu.make_async_copy(sent_a, sent_a, msend_sem).wait()
    pltpu.make_async_copy(sent_b, sent_b, nsend_sem).wait()


def permuted(values, in_rows, out_rows, first, second):
    first[...] = jnp.concatenate([values.astype(F32), jnp.zeros((112, 128), F32)], axis=0).T
    for k in range(8):
        second[out_rows(k), :] = first[in_rows(k), :]
    return second[...].T[0:16].astype(I32)


def finish(level_in, msg_in, bld_ref, expo_in, level_ref, build_ref, expo_ref, first, second, sems):
    pieces = []
    for k in range(4):
        cut = pl.ds(k * (WIDTH // 4), WIDTH // 4)
        pieces.append(pltpu.make_async_copy(expo_in.at[cut], expo_ref.at[cut], sems.at[k]))
        pieces[k].start()
    level_ref[...] = level_in[...]
    got = msg_in[...].reshape(128, 128).T
    bld = permuted(
        bld_ref[...], lambda k: pl.ds(k // 2 * 32 + k % 2, 16, stride=2), lambda k: pl.ds(k, 16, stride=8), first, second
    )
    bld_high, bld_low = bld // 128, bld % 128
    sub = lax.broadcasted_iota(I32, (128, 128), 0)
    lhs, hots = [], []
    for c in range(CAP_ADDR):
        mine = lax.broadcasted_iota(I32, (16, 128), 0) == bld_high[c : c + 1]
        spread = jnp.where(mine, got[c : c + 1], 0.0)
        count = jnp.where(mine, got[16 + c : 17 + c], 0.0)
        lhs.append(jnp.concatenate([*split3(spread), count.astype(BF16)], axis=0))
        hots.append(jnp.where(sub == bld_low[c : c + 1], 1.0, 0.0).astype(BF16))
    sums = lax.dot_general(
        jnp.concatenate(lhs, axis=1), jnp.concatenate(hots, axis=1), (((1,), (1,)), ((), ())), preferred_element_type=F32
    )
    build_ref[...] = (sums[0:16] + sums[16:32] + sums[32:48]) / jnp.maximum(sums[48:64], 1.0)
    for piece in pieces:
        piece.wait()


def local(emission, path_sends, tile_slots, geometry, absorption, hour_period, dwellings, addr_sends, addr_building):
    vmem = pl.BlockSpec(memory_space=pltpu.VMEM)
    level, messages, exposure = pl.pallas_call(
        kernel,
        out_shape=(
            jax.ShapeDtypeStruct((16, 128), F32),
            jax.ShapeDtypeStruct((16, 8, 128), F32),
            jax.ShapeDtypeStruct((WIDTH, TILE_DEV * RECV_TILE), F32),
        ),
        in_specs=[vmem, vmem, vmem, pl.BlockSpec(memory_space=pl.ANY), vmem, pl.BlockSpec(memory_space=pltpu.SMEM), vmem, vmem],
        out_specs=(vmem, vmem, vmem),
        scratch_shapes=[
            pltpu.VMEM((SEG_DEV, 256), BF16),
            pltpu.VMEM((DEVICES, BLOCK, 128), BF16),
            pltpu.VMEM((DEVICES, BLOCK, 128), BF16),
            pltpu.VMEM((GROUP * CAP, 256), BF16),
            pltpu.VMEM((PATHS, 256), F32),
            pltpu.VMEM((PATHS, 128), BF16),
            pltpu.VMEM((PATHS, 128), BF16),
            pltpu.VMEM((TILE_DEV, RECV_TILE, PATHS_TILE), BF16),
            pltpu.VMEM((WIDTH, 128), F32),
            pltpu.VMEM((128, 128), F32),
            pltpu.VMEM((128, 128), F32),
            pltpu.VMEM((128, 2048), BF16),
            pltpu.VMEM((8, 16, 128), F32),
            pltpu.VMEM((8, 16, 128), F32),
            pltpu.VMEM((16, 8, 128), F32),
            pltpu.VMEM((16, 8, 128), F32),
            pltpu.SemaphoreType.DMA,
            pltpu.SemaphoreType.DMA,
            pltpu.SemaphoreType.DMA,
            pltpu.SemaphoreType.DMA((DEVICES // GROUP,)),
            pltpu.SemaphoreType.DMA,
            pltpu.SemaphoreType.DMA,
            pltpu.SemaphoreType.DMA((2,)),
        ],
        compiler_params=pltpu.CompilerParams(collective_id=0, has_side_effects=True, vmem_limit_bytes=56 * 2**20),
        name="noise_map",
    )(
        emission.T,
        path_sends[0].T,
        tile_slots,
        geometry,
        absorption,
        hour_period,
        dwellings.reshape(16, 128),
        addr_sends[0].T,
    )
    hbm = pl.BlockSpec(memory_space=pl.ANY)
    level, building, exposure = pl.pallas_call(
        finish,
        out_shape=(
            jax.ShapeDtypeStruct((16, 128), F32),
            jax.ShapeDtypeStruct((16, 128), F32),
            jax.ShapeDtypeStruct((WIDTH, TILE_DEV * RECV_TILE), F32),
        ),
        in_specs=[vmem, vmem, vmem, hbm],
        out_specs=(vmem, vmem, hbm),
        scratch_shapes=[pltpu.VMEM((128, 128), F32), pltpu.VMEM((128, 128), F32), pltpu.SemaphoreType.DMA((4,))],
        compiler_params=pltpu.CompilerParams(vmem_limit_bytes=16 * 2**20),
        name="buildings",
    )(level, messages, addr_building[0].T, exposure)
    return level.reshape(-1), building.reshape(-1), exposure.T


def solution(mesh):
    both = ("region", "band")
    in_specs = (P(both, None), P(both, None, None), P(both, None), P(both, None, None), P(both, None, None), P(), P(both), P(both, None, None), P(both, None, None))
    out_specs = (P(both), P(both), P(both, None))
    return jax.shard_map(local, mesh=mesh, in_specs=in_specs, out_specs=out_specs, check_vma=False)
```

```python
import math

import jax
import jax.numpy as jnp
from jax import lax
from jax.experimental import pallas as pl
from jax.experimental.pallas import tpu as pltpu
from jax.sharding import PartitionSpec as P

BANDS = 8
HOURS = 24
WIDTH = BANDS * HOURS
SEG_DEV = 512
CAP = 64
TILE_DEV = 8
RECV_TILE = 256
PATHS_TILE = 512
CAP_ADDR = 16
DEVICES = 128
PATHS = TILE_DEV * PATHS_TILE
PART = 64
STRIDE = (16, 4, 1)
PLANE = ((1, 2), (0, 2), (0, 1))
SPAN = 4096
LAG = 2
A_WEIGHTING_DB = (-26.2, -16.1, -8.6, -3.2, 0.0, 1.2, 1.0, -1.1)
MESH = pl.DeviceIdType.MESH
BF16, F32, I32 = jnp.bfloat16, jnp.float32, jnp.int32


def split3(value):
    high = value.astype(BF16)
    rest = value - high.astype(F32)
    mid = rest.astype(BF16)
    return high, mid, (rest - mid.astype(F32)).astype(BF16)


def my_place():
    region, core = lax.axis_index("region"), lax.axis_index("band")
    return (region // 16, (region // 4) % 4, region % 4), core


def one_hot(row, count):
    lines = lax.broadcasted_iota(I32, (count, row.shape[1]), 0)
    return jnp.where(lines == row, 1.0, 0.0).astype(BF16)


def drain(ref, sem):
    pltpu.make_async_copy(ref, ref, sem).wait()


def kernel(
    em_ref, ps_ref, slot_ref, geo_hbm, abs_ref, hour_ref, dwell_ref, addr_ref,
    level_ref, msg_ref, expo_ref,
    even, odd, lines, lists, outb, recv, acc, label, quarter, geo, weight, first, second, hots, out_a, in_a, out_b, in_b,
    geo_sem, line_sem, list_sem, send_sem, line_in, list_in, recv_sem, msend_sem, nsend_sem, mrecv_sem,
):
    at, core = my_place()
    y, x, z = at
    geo_copy = pltpu.make_async_copy(geo_hbm, geo, geo_sem)
    geo_copy.start()
    barrier = pltpu.get_barrier_semaphore()
    peers = 0
    for dy in range(4):
        for dx in range(4):
            for dz in range(4):
                for dc in range(2):
                    if 0 in (dy, dx, dz) and (dy, dx, dz, dc) != (0, 0, 0, 0):
                        to = ((y + dy) % 4) * 16 + ((x + dx) % 4) * 4 + (z + dz) % 4
                        pl.semaphore_signal(barrier, inc=1, device_id=(to, (core + dc) % 2), device_id_type=MESH)
                        peers += 1

    entries = ps_ref[...].astype(F32)
    first[...] = jnp.concatenate([entries, entries], axis=0).T
    zero, one = first[pl.ds(0, 64, stride=2), :], first[pl.ds(1, 64, stride=2), :]
    left = lax.broadcasted_iota(I32, (64, 128), 1) < 64
    both, swapped = jnp.where(left, zero, one), jnp.where(left, one, zero)
    for a in range(4):
        for b in range(4):
            cut = slice((a * 4 + b) * 4, (a * 4 + b) * 4 + 4)
            even[a, b, :, 0, :] = both[cut]
            odd[a, b, :, 0, :] = swapped[cut]

    pl.semaphore_wait(barrier, peers)

    def plane_of(ref, p, where):
        return ref.at[where] if p == 0 else ref.at[:, where] if p == 1 else ref.at[:, :, where]

    for j in (1, 3, 2):
        for p in range(3):
            where = (at[p] + j) % 4
            to = sum(STRIDE[q] * (where if q == p else at[q]) for q in range(3))
            pltpu.make_async_remote_copy(
                src_ref=plane_of(odd if j % 2 else even, p, where), dst_ref=lists.at[p * 4 + j],
                send_sem=list_sem, recv_sem=list_in.at[p], device_id=(to, core), device_id_type=MESH,
            ).start()
            pltpu.make_async_remote_copy(
                src_ref=em_ref.at[pl.ds(p * PART, PART)], dst_ref=lines.at[p * 4 + j],
                send_sem=line_sem, recv_sem=line_in.at[p], device_id=(to, core), device_id_type=MESH,
            ).start()
    for p in range(3):
        lines[p * 4] = em_ref[p * PART : (p + 1) * PART, :]
        lists[p * 4] = plane_of(even, p, at[p])[...]

    def pick(u, carry):
        for p in range(3):
            b1, b2 = PLANE[p]
            line1 = (at[b1] + u) % 4
            line2 = [(at[b2] + v) % 4 for v in range(4)]

            @pl.when(u == 0)
            def _():
                drain(lists.at[pl.ds(p * 4 + 1, 3)], list_in.at[p])
                drain(lines.at[pl.ds(p * 4 + 1, 3)], line_in.at[p])

            found = []
            for i in range(4):
                row = jnp.concatenate([lists[p * 4 + i, line1, v] for v in line2], axis=1)
                upper = row >= 256.0
                table = one_hot(jnp.where(upper, row - 256.0, row).astype(I32), 256)
                source = lines[p * 4 + i]
                halves = jnp.concatenate([source[:, 0:256], source[:, 256:512]], axis=0)
                out = jnp.dot(halves, table, preferred_element_type=F32)
                found.append(jnp.where(upper, out[PART:], out[:PART]))
            low = lax.broadcasted_iota(I32, (PART, 512), 1) % 128 < 64
            for k in range(2):
                pairs = []
                for i in (0, 2):
                    a, b = (found[i], found[i + 1]) if k == 0 else (found[i + 1], found[i])
                    pairs.append(jnp.where(low, a, b).astype(BF16))
                for v in range(4):
                    cut = slice(v * 128, (v + 1) * 128)
                    outb[(p * 4 + u) * 8 + k * 4 + v] = jnp.concatenate([pairs[0][:, cut], pairs[1][:, cut]], axis=1)
            for dc in range(2):
                to_core = (core + dc) % 2
                for v in range(4):
                    to = STRIDE[p] * at[p] + STRIDE[b1] * line1 + STRIDE[b2] * line2[v]
                    copy = pltpu.make_async_remote_copy(
                        src_ref=outb.at[(p * 4 + u) * 8 + to_core * 4 + v], dst_ref=recv.at[(p * 4 + u) * 8 + dc * 4 + v],
                        send_sem=send_sem, recv_sem=recv_sem.at[p * 4 + u], device_id=(to, to_core), device_id_type=MESH,
                    )
                    if dc or v:
                        copy.start()
                    else:

                        @pl.when(u > 0)
                        def _():
                            copy.start()

                        @pl.when(u == 0)
                        def _():
                            recv[p * 32] = outb[p * 32 + core * 4]

        return carry

    slots = slot_ref[...]
    safe = jnp.maximum(slots, 0)
    source, entry = safe // CAP, safe % CAP
    apart = (
        (y + 4 - source // 32) % 4, (x + 4 - (source // 8) % 4) % 4, (z + 4 - (source // 2) % 4) % 4,
    )
    other = (core + 2 - source % 2) % 2
    for p in range(3):
        b1, b2 = PLANE[p]
        lane = (apart[p] // 2) * 128 + ((apart[p] + core) % 2) * 64 + entry
        group = jnp.where(slots >= 0, apart[b1] * 2 + other, -1)
        for g in range(8):
            label[p * 8 + g] = jnp.where(group == g, lane, -1)
        quarter[p] = apart[b2]

    r = lax.broadcasted_iota(I32, (WIDTH, 128), 0)
    scale = jnp.zeros((WIDTH, 128), F32)
    for b in range(BANDS):
        scale = jnp.where(r // HOURS == b, jnp.float32(10.0 ** (A_WEIGHTING_DB[b] / 10.0)), scale)
    gain = jnp.zeros((WIDTH, 128), F32)
    for h in range(HOURS):
        period = hour_ref[h]
        g = jnp.where(period == 0, 1.0, jnp.where(period == 1, jnp.float32(10.0**0.5), jnp.where(period == 2, 10.0, 0.0)))
        gain = jnp.where(r % HOURS == h, g.astype(F32), gain)
    weight[...] = scale * gain / HOURS

    addr = permuted(
        addr_ref[...], lambda k: pl.ds(k // 2 * 32 + k % 2, 16, stride=2), lambda k: pl.ds(k * 16, 16), first, second
    )
    addr_high = jnp.maximum(addr, 0) // 128
    addr_low = jnp.where(addr >= 0, addr % 128, -1)
    for c in range(CAP_ADDR):
        hots[:, c * 128 : (c + 1) * 128] = one_hot(addr_low[c : c + 1], 128)
    acc[...] = jnp.zeros_like(acc)

    def gather(u, carry):
        for p in range(3):
            step = p * 4 + u

            @pl.when(u == 0)
            def _():
                drain(recv.at[pl.ds(p * 32 + 1, 7)], recv_sem.at[step])

            @pl.when(u > 0)
            def _():
                drain(recv.at[pl.ds(step * 8, 8)], recv_sem.at[step])

            def some_paths(n, inner):
                def row_of(ref, index):
                    first_tile = n * (SPAN // PATHS_TILE)
                    return jnp.concatenate([ref[index, pl.ds(first_tile + m, 1), :] for m in range(SPAN // PATHS_TILE)], axis=1)

                table = jnp.concatenate([one_hot(row_of(label, p * 8 + u * 2 + dc), 256) for dc in range(2)], axis=0)
                data = jnp.concatenate(
                    [recv[pl.ds(step * 8 + dc * 4, 4)].reshape(4 * PART, 256) for dc in range(2)], axis=1
                )
                out = jnp.dot(data, table, preferred_element_type=F32)
                which = row_of(quarter, p)
                out = [out[v * PART : (v + 1) * PART] for v in range(4)]
                mine = jnp.where(which < 2, jnp.where(which == 0, out[0], out[1]), jnp.where(which == 2, out[2], out[3]))
                cut = (slice(p * PART, (p + 1) * PART), pl.ds(pl.multiple_of(n * SPAN, SPAN), SPAN))
                acc[cut] = acc[cut] + mine
                return inner

            lax.fori_loop(0, PATHS // SPAN, some_paths, 0)
        return carry

    def turn(u, carry):
        @pl.when(u < 4)
        def _():
            pick(u, 0)

        @pl.when(u >= LAG)
        def _():
            gather(u - LAG, 0)

        return carry

    lax.fori_loop(0, 4 + LAG, turn, 0)
    geo_copy.wait()

    def tile(t, carry):
        gathered = acc[:, pl.ds(pl.multiple_of(t * PATHS_TILE, PATHS_TILE), PATHS_TILE)]
        damp = abs_ref[t].astype(F32)
        factor = jnp.concatenate(
            [jnp.broadcast_to(damp[b : b + 1], (HOURS, PATHS_TILE)) for b in range(BANDS)], axis=0
        )
        mixed = (factor * gathered).astype(BF16)
        exposure = lax.dot_general(mixed, geo[t], (((1,), (1,)), ((), ())), preferred_element_type=F32)
        expo_ref[:, pl.ds(pl.multiple_of(t * RECV_TILE, RECV_TILE), RECV_TILE)] = exposure
        for half in range(2):
            energy = jnp.sum(exposure[:, half * 128 : (half + 1) * 128] * weight[...], axis=0, keepdims=True)
            level_ref[pl.ds(2 * t + half, 1), :] = jnp.log(energy) * jnp.float32(1.0 / math.log(10.0))
        return carry

    lax.fori_loop(0, TILE_DEV, tile, 0)

    dwell = dwell_ref[...].astype(F32)
    table = jnp.concatenate([*split3(dwell * level_ref[...]), dwell.astype(BF16)], axis=0)
    found = jnp.dot(table, hots[...], preferred_element_type=F32)
    level_rows = found[0:16] + found[16:32] + found[32:48]
    weighted, dwelt = [], []
    for c in range(CAP_ADDR):
        lanes = slice(c * 128, (c + 1) * 128)
        mine = lax.broadcasted_iota(I32, (16, 128), 0) == addr_high[c : c + 1]
        weighted.append(jnp.sum(jnp.where(mine, level_rows[:, lanes], 0.0), axis=0, keepdims=True))
        dwelt.append(jnp.sum(jnp.where(mine, found[48:64, lanes], 0.0), axis=0, keepdims=True))
    out_a[...] = jnp.concatenate(weighted + dwelt + [jnp.zeros((96, 128), F32)], axis=0).T.reshape(8, 16, 128)
    mine_a, mine_b = y * 2 + core, x * 4 + z
    in_a[mine_a] = out_a[mine_a]
    for k in range(1, 8):
        to_y, to_core = (y + k // 2) % 4, (core + k % 2) % 2
        pltpu.make_async_remote_copy(
            src_ref=out_a.at[to_y * 2 + to_core], dst_ref=in_a.at[mine_a], send_sem=msend_sem, recv_sem=mrecv_sem.at[0],
            device_id=(to_y * 16 + mine_b, to_core), device_id_type=MESH,
        ).start()
    seven = in_a.at[pl.ds(0, 7)]
    pltpu.make_async_copy(seven, seven, mrecv_sem.at[0]).wait()
    for k in range(8):
        out_b[:, k, :] = in_a[k]
    in_b[mine_b] = out_b[mine_b]
    for k in range(1, 16):
        to = ((x + k // 4) % 4) * 4 + (z + k % 4) % 4
        pltpu.make_async_remote_copy(
            src_ref=out_b.at[to], dst_ref=in_b.at[mine_b], send_sem=nsend_sem, recv_sem=mrecv_sem.at[1],
            device_id=(y * 16 + to, core), device_id_type=MESH,
        ).start()
    fifteen = in_b.at[pl.ds(0, 15)]
    pltpu.make_async_copy(fifteen, fifteen, mrecv_sem.at[1]).wait()
    msg_ref[...] = in_b[...]

    drain(lists.at[pl.ds(0, 9)], list_sem)
    drain(lines.at[pl.ds(0, 9)], line_sem)
    drain(outb.at[pl.ds(0, 93)], send_sem)
    drain(out_a.at[pl.ds(0, 7)], msend_sem)
    drain(out_b.at[pl.ds(0, 15)], nsend_sem)


def permuted(values, in_rows, out_rows, first, second):
    first[...] = jnp.concatenate([values.astype(F32), jnp.zeros((112, 128), F32)], axis=0).T
    for k in range(8):
        second[out_rows(k), :] = first[in_rows(k), :]
    return second[...].T[0:16].astype(I32)


def finish(level_in, msg_in, bld_ref, expo_in, level_ref, build_ref, expo_ref, first, second, sems):
    pieces = []
    for k in range(4):
        cut = pl.ds(k * (WIDTH // 4), WIDTH // 4)
        pieces.append(pltpu.make_async_copy(expo_in.at[cut], expo_ref.at[cut], sems.at[k]))
        pieces[k].start()
    level_ref[...] = level_in[...]
    got = msg_in[...].reshape(128, 128).T
    bld = permuted(
        bld_ref[...], lambda k: pl.ds(k // 2 * 32 + k % 2, 16, stride=2), lambda k: pl.ds(k, 16, stride=8), first, second
    )
    bld_high, bld_low = bld // 128, bld % 128
    sub = lax.broadcasted_iota(I32, (128, 128), 0)
    lhs, hots = [], []
    for c in range(CAP_ADDR):
        mine = lax.broadcasted_iota(I32, (16, 128), 0) == bld_high[c : c + 1]
        spread = jnp.where(mine, got[c : c + 1], 0.0)
        count = jnp.where(mine, got[16 + c : 17 + c], 0.0)
        lhs.append(jnp.concatenate([*split3(spread), count.astype(BF16)], axis=0))
        hots.append(jnp.where(sub == bld_low[c : c + 1], 1.0, 0.0).astype(BF16))
    sums = lax.dot_general(
        jnp.concatenate(lhs, axis=1), jnp.concatenate(hots, axis=1), (((1,), (1,)), ((), ())), preferred_element_type=F32
    )
    build_ref[...] = (sums[0:16] + sums[16:32] + sums[32:48]) / jnp.maximum(sums[48:64], 1.0)
    for piece in pieces:
        piece.wait()


def local(emission, path_sends, tile_slots, geometry, absorption, hour_period, dwellings, addr_sends, addr_building):
    vmem = pl.BlockSpec(memory_space=pltpu.VMEM)
    level, messages, exposure = pl.pallas_call(
        kernel,
        out_shape=(
            jax.ShapeDtypeStruct((16, 128), F32),
            jax.ShapeDtypeStruct((16, 8, 128), F32),
            jax.ShapeDtypeStruct((WIDTH, TILE_DEV * RECV_TILE), F32),
        ),
        in_specs=[vmem, vmem, vmem, pl.BlockSpec(memory_space=pl.ANY), vmem, pl.BlockSpec(memory_space=pltpu.SMEM), vmem, vmem],
        out_specs=(vmem, vmem, vmem),
        scratch_shapes=[
            pltpu.VMEM((4, 4, 4, 1, 128), F32),
            pltpu.VMEM((4, 4, 4, 1, 128), F32),
            pltpu.VMEM((12, PART, SEG_DEV), BF16),
            pltpu.VMEM((12, 4, 4, 1, 128), F32),
            pltpu.VMEM((96, PART, 256), BF16),
            pltpu.VMEM((96, PART, 256), BF16),
            pltpu.VMEM((WIDTH, PATHS), F32),
            pltpu.VMEM((24, TILE_DEV, PATHS_TILE), I32),
            pltpu.VMEM((3, TILE_DEV, PATHS_TILE), I32),
            pltpu.VMEM((TILE_DEV, RECV_TILE, PATHS_TILE), BF16),
            pltpu.VMEM((WIDTH, 128), F32),
            pltpu.VMEM((128, 128), F32),
            pltpu.VMEM((128, 128), F32),
            pltpu.VMEM((128, 2048), BF16),
            pltpu.VMEM((8, 16, 128), F32),
            pltpu.VMEM((8, 16, 128), F32),
            pltpu.VMEM((16, 8, 128), F32),
            pltpu.VMEM((16, 8, 128), F32),
            pltpu.SemaphoreType.DMA,
            pltpu.SemaphoreType.DMA,
            pltpu.SemaphoreType.DMA,
            pltpu.SemaphoreType.DMA,
            pltpu.SemaphoreType.DMA((3,)),
            pltpu.SemaphoreType.DMA((3,)),
            pltpu.SemaphoreType.DMA((12,)),
            pltpu.SemaphoreType.DMA,
            pltpu.SemaphoreType.DMA,
            pltpu.SemaphoreType.DMA((2,)),
        ],
        compiler_params=pltpu.CompilerParams(collective_id=0, has_side_effects=True, vmem_limit_bytes=56 * 2**20),
        name="noise_map",
    )(
        emission.T,
        path_sends[0].T,
        tile_slots,
        geometry,
        absorption,
        hour_period,
        dwellings.reshape(16, 128),
        addr_sends[0].T,
    )
    hbm = pl.BlockSpec(memory_space=pl.ANY)
    level, building, exposure = pl.pallas_call(
        finish,
        out_shape=(
            jax.ShapeDtypeStruct((16, 128), F32),
            jax.ShapeDtypeStruct((16, 128), F32),
            jax.ShapeDtypeStruct((WIDTH, TILE_DEV * RECV_TILE), F32),
        ),
        in_specs=[vmem, vmem, vmem, hbm],
        out_specs=(vmem, vmem, hbm),
        scratch_shapes=[pltpu.VMEM((128, 128), F32), pltpu.VMEM((128, 128), F32), pltpu.SemaphoreType.DMA((4,))],
        compiler_params=pltpu.CompilerParams(vmem_limit_bytes=16 * 2**20),
        name="buildings",
    )(level, messages, addr_building[0].T, exposure)
    return level.reshape(-1), building.reshape(-1), exposure.T


def solution(mesh):
    both = ("region", "band")
    in_specs = (P(both, None), P(both, None, None), P(both, None), P(both, None, None), P(both, None, None), P(), P(both), P(both, None, None), P(both, None, None))
    out_specs = (P(both), P(both), P(both, None))
    return jax.shard_map(local, mesh=mesh, in_specs=in_specs, out_specs=out_specs, check_vma=False)
```

```python
import math

import jax
import jax.numpy as jnp
from jax import lax
from jax.experimental import pallas as pl
from jax.experimental.pallas import tpu as pltpu
from jax.sharding import PartitionSpec as P

BANDS = 8
HOURS = 24
WIDTH = BANDS * HOURS
SEG_DEV = 512
CAP = 64
TILE_DEV = 8
RECV_TILE = 256
PATHS_TILE = 512
CAP_ADDR = 16
DEVICES = 128
PATHS = TILE_DEV * PATHS_TILE
PART = 64
STRIDE = (16, 4, 1)
PLANE = ((1, 2), (0, 2), (0, 1))
SPAN = 4096
CUTS = 6
AHEAD = 7
A_WEIGHTING_DB = (-26.2, -16.1, -8.6, -3.2, 0.0, 1.2, 1.0, -1.1)
MESH = pl.DeviceIdType.MESH
BF16, F32, I32 = jnp.bfloat16, jnp.float32, jnp.int32


def split3(value):
    high = value.astype(BF16)
    rest = value - high.astype(F32)
    mid = rest.astype(BF16)
    return high, mid, (rest - mid.astype(F32)).astype(BF16)


def my_place():
    region, core = lax.axis_index("region"), lax.axis_index("band")
    return (region // 16, (region // 4) % 4, region % 4), core


def one_hot(row, count):
    lines = lax.broadcasted_iota(I32, (count, row.shape[1]), 0)
    return jnp.where(lines == row, 1.0, 0.0).astype(BF16)


def drain(ref, sem):
    pltpu.make_async_copy(ref, ref, sem).wait()


def kernel(
    em_hbm, ps_hbm, slot_hbm, geo_hbm, abs_hbm, hour_hbm, dwell_hbm, addr_hbm,
    small_ref, expo_hbm,
    ps_ref, slot_ref, abs_ref, hour_ref, dwell_ref, addr_ref, expo_ref, even, odd, lines, lists, outb, recv, acc, label, sender, geo, weight, first, second, hots, out_a, in_a, out_b, in_b,
    in_sem, own_sem, out_sem, geo_sem, line_sem, list_sem, send_sem, line_in, list_in, recv_sem, msend_sem, nsend_sem, mrecv_sem,
):
    at, core = my_place()
    y, x, z = at
    inputs = ((ps_hbm, ps_ref), (slot_hbm, slot_ref), (abs_hbm, abs_ref), (hour_hbm, hour_ref), (dwell_hbm, dwell_ref), (addr_hbm, addr_ref))
    inputs = [pltpu.make_async_copy(a, b, in_sem.at[k]) for k, (a, b) in enumerate(inputs)]
    for copy in inputs:
        copy.start()
    own_lines = [pltpu.make_async_copy(em_hbm.at[pl.ds(p * PART, PART)], lines.at[p * 4], own_sem.at[p]) for p in range(3)]
    for copy in own_lines:
        copy.start()
    geo_copy = pltpu.make_async_copy(geo_hbm, geo, geo_sem)
    geo_copy.start()
    barrier = pltpu.get_barrier_semaphore()
    peers = 0
    for dy in range(4):
        for dx in range(4):
            for dz in range(4):
                for dc in range(2):
                    if 0 in (dy, dx, dz) and (dy, dx, dz, dc) != (0, 0, 0, 0):
                        to = ((y + dy) % 4) * 16 + ((x + dx) % 4) * 4 + (z + dz) % 4
                        pl.semaphore_signal(barrier, inc=1, device_id=(to, (core + dc) % 2), device_id_type=MESH)
                        peers += 1

    inputs[0].wait()
    entries = ps_ref[...].astype(F32)
    first[...] = jnp.concatenate([entries, entries], axis=0).T
    zero, one = first[pl.ds(0, 64, stride=2), :], first[pl.ds(1, 64, stride=2), :]
    left = lax.broadcasted_iota(I32, (64, 128), 1) < 64
    both, swapped = jnp.where(left, zero, one), jnp.where(left, one, zero)
    for a in range(4):
        for b in range(4):
            cut = slice((a * 4 + b) * 4, (a * 4 + b) * 4 + 4)
            even[a, b, :, 0, :] = both[cut]
            odd[a, b, :, 0, :] = swapped[cut]

    pl.semaphore_wait(barrier, peers)

    def plane_of(ref, p, where):
        return ref.at[where] if p == 0 else ref.at[:, where] if p == 1 else ref.at[:, :, where]

    for j in (1, 3, 2):
        for p in range(3):
            where = (at[p] + j) % 4
            to = sum(STRIDE[q] * (where if q == p else at[q]) for q in range(3))
            pltpu.make_async_remote_copy(
                src_ref=plane_of(odd if j % 2 else even, p, where), dst_ref=lists.at[p * 4 + j],
                send_sem=list_sem, recv_sem=list_in.at[p], device_id=(to, core), device_id_type=MESH,
            ).start()
            pltpu.make_async_remote_copy(
                src_ref=em_hbm.at[pl.ds(p * PART, PART)], dst_ref=lines.at[p * 4 + j],
                send_sem=line_sem, recv_sem=line_in.at[p], device_id=(to, core), device_id_type=MESH,
            ).start()
    for p in range(3):
        lists[p * 4] = plane_of(even, p, at[p])[...]
        own_lines[p].wait()
    for copy in inputs[1:]:
        copy.wait()

    def pick(u, p):
        b1, b2 = PLANE[p]
        line1 = [(at[b1] + u + 4 - v) % 4 for v in range(4)]
        line2 = [(at[b2] + v) % 4 for v in range(4)]

        @pl.when(u == 0)
        def _():
            drain(lists.at[pl.ds(p * 4 + 1, 3)], list_in.at[p])
            drain(lines.at[pl.ds(p * 4 + 1, 3)], line_in.at[p])

        found = []
        for i in range(4):
            row = jnp.concatenate([lists[p * 4 + i, line1[v], line2[v]] for v in range(4)], axis=1)
            upper = row >= 256.0
            table = one_hot(jnp.where(upper, row - 256.0, row).astype(I32), 256)
            source = lines[p * 4 + i]
            halves = jnp.concatenate([source[:, 0:256], source[:, 256:512]], axis=0)
            out = jnp.dot(halves, table, preferred_element_type=F32)
            found.append(jnp.where(upper, out[PART:], out[:PART]))
        low = lax.broadcasted_iota(I32, (PART, 512), 1) % 128 < 64
        for k in range(2):
            pairs = []
            for i in (0, 2):
                a, b = (found[i], found[i + 1]) if k == 0 else (found[i + 1], found[i])
                pairs.append(jnp.where(low, a, b).astype(BF16))
            for v in range(4):
                cut = slice(v * 128, (v + 1) * 128)
                outb[(p * 4 + u) * 8 + k * 4 + v] = jnp.concatenate([pairs[0][:, cut], pairs[1][:, cut]], axis=1)
        for dc in range(2):
            to_core = (core + dc) % 2
            for v in range(4):
                to = STRIDE[p] * at[p] + STRIDE[b1] * line1[v] + STRIDE[b2] * line2[v]
                copy = pltpu.make_async_remote_copy(
                    src_ref=outb.at[(p * 4 + u) * 8 + to_core * 4 + v], dst_ref=recv.at[(p * 4 + u) * 8 + dc * 4 + v],
                    send_sem=send_sem, recv_sem=recv_sem.at[p * 4 + u], device_id=(to, to_core), device_id_type=MESH,
                )
                if dc or v:
                    copy.start()
                else:

                    @pl.when(u > 0)
                    def _():
                        copy.start()

                    @pl.when(u == 0)
                    def _():
                        recv[p * 32] = outb[p * 32 + core * 4]

    slots = slot_ref[...]
    safe = jnp.maximum(slots, 0)
    source, entry = safe // CAP, safe % CAP
    apart = (
        (y + 4 - source // 32) % 4, (x + 4 - (source // 8) % 4) % 4, (z + 4 - (source // 2) % 4) % 4,
    )
    other = (core + 2 - source % 2) % 2
    for p in range(3):
        b1, b2 = PLANE[p]
        lane = (apart[p] // 2) * 128 + ((apart[p] + core) % 2) * 64 + entry
        group = jnp.where(slots >= 0, (apart[b1] + apart[b2]) % 4, -1)
        for g in range(4):
            label[p * 4 + g] = jnp.where(group == g, lane, -1)
        sender[p] = other * 4 + apart[b2]

    r = lax.broadcasted_iota(I32, (WIDTH, 128), 0)
    scale = jnp.zeros((WIDTH, 128), F32)
    for b in range(BANDS):
        scale = jnp.where(r // HOURS == b, jnp.float32(10.0 ** (A_WEIGHTING_DB[b] / 10.0)), scale)
    gain = jnp.zeros((WIDTH, 128), F32)
    for h in range(HOURS):
        period = hour_ref[h]
        g = jnp.where(period == 0, 1.0, jnp.where(period == 1, jnp.float32(10.0**0.5), jnp.where(period == 2, 10.0, 0.0)))
        gain = jnp.where(r % HOURS == h, g.astype(F32), gain)
    weight[...] = scale * gain / HOURS

    addr = permuted(
        addr_ref[...], lambda k: pl.ds(k // 2 * 32 + k % 2, 16, stride=2), lambda k: pl.ds(k * 16, 16), first, second
    )
    addr_high = jnp.maximum(addr, 0) // 128
    addr_low = jnp.where(addr >= 0, addr % 128, -1)
    for c in range(CAP_ADDR):
        hots[:, c * 128 : (c + 1) * 128] = one_hot(addr_low[c : c + 1], 128)
    acc[...] = jnp.zeros_like(acc)

    def gather(u, p):
        step = p * 4 + u

        @pl.when(u == 0)
        def _():
            drain(recv.at[pl.ds(p * 32 + 1, 7)], recv_sem.at[step])

        @pl.when(u > 0)
        def _():
            drain(recv.at[pl.ds(step * 8, 8)], recv_sem.at[step])

        def some_paths(n, inner):
            def row_of(ref, index):
                first_tile = n * (SPAN // PATHS_TILE)
                return jnp.concatenate([ref[index, pl.ds(first_tile + m, 1), :] for m in range(SPAN // PATHS_TILE)], axis=1)

            table = one_hot(row_of(label, step), 256)
            data = recv[pl.ds(step * 8, 8)].reshape(8 * PART, 256)
            out = jnp.dot(data, table, preferred_element_type=F32)
            which = row_of(sender, p)
            mine = out[0:PART]
            for k in range(1, 8):
                mine = jnp.where(which == k, out[k * PART : (k + 1) * PART], mine)
            cut = (slice(p * PART, (p + 1) * PART), pl.ds(pl.multiple_of(n * SPAN, SPAN), SPAN))
            acc[cut] = acc[cut] + mine
            return inner

        lax.fori_loop(0, PATHS // SPAN, some_paths, 0)

    def turn(u, carry):
        for p in range(3):

            @pl.when(u < 4)
            def _():
                pick(u, p)

            late = (p - AHEAD) % 3
            back = (AHEAD + late - p) // 3

            @pl.when((u >= back) & (u < 4 + back))
            def _():
                gather(u - back, late)

        return carry

    lax.fori_loop(0, 4 + (AHEAD + 2) // 3, turn, 0)
    geo_copy.wait()

    def tile(t, carry):
        gathered = acc[:, pl.ds(pl.multiple_of(t * PATHS_TILE, PATHS_TILE), PATHS_TILE)]
        damp = abs_ref[t].astype(F32)
        factor = jnp.concatenate(
            [jnp.broadcast_to(damp[b : b + 1], (HOURS, PATHS_TILE)) for b in range(BANDS)], axis=0
        )
        mixed = (factor * gathered).astype(BF16)
        exposure = lax.dot_general(mixed, geo[t], (((1,), (1,)), ((), ())), preferred_element_type=F32)
        expo_ref[:, pl.ds(pl.multiple_of(t * RECV_TILE, RECV_TILE), RECV_TILE)] = exposure
        for half in range(2):
            energy = jnp.sum(exposure[:, half * 128 : (half + 1) * 128] * weight[...], axis=0, keepdims=True)
            small_ref[pl.ds(2 * t + half, 1), :] = jnp.log(energy) * jnp.float32(1.0 / math.log(10.0))
        return carry

    lax.fori_loop(0, TILE_DEV, tile, 0)

    expo_copy = pltpu.make_async_copy(expo_ref, expo_hbm, out_sem)
    expo_copy.start()
    dwell = dwell_ref[...].astype(F32)
    table = jnp.concatenate([*split3(dwell * small_ref[0:16, :]), dwell.astype(BF16)], axis=0)
    found = jnp.dot(table, hots[...], preferred_element_type=F32)
    level_rows = found[0:16] + found[16:32] + found[32:48]
    weighted, dwelt = [], []
    for c in range(CAP_ADDR):
        lanes = slice(c * 128, (c + 1) * 128)
        mine = lax.broadcasted_iota(I32, (16, 128), 0) == addr_high[c : c + 1]
        weighted.append(jnp.sum(jnp.where(mine, level_rows[:, lanes], 0.0), axis=0, keepdims=True))
        dwelt.append(jnp.sum(jnp.where(mine, found[48:64, lanes], 0.0), axis=0, keepdims=True))
    out_a[...] = jnp.concatenate(weighted + dwelt + [jnp.zeros((96, 128), F32)], axis=0).T.reshape(8, 16, 128)
    mine_a, mine_b = y * 2 + core, x * 4 + z
    in_a[mine_a] = out_a[mine_a]
    for k in range(1, 8):
        to_y, to_core = (y + k // 2) % 4, (core + k % 2) % 2
        pltpu.make_async_remote_copy(
            src_ref=out_a.at[to_y * 2 + to_core], dst_ref=in_a.at[mine_a], send_sem=msend_sem, recv_sem=mrecv_sem.at[0],
            device_id=(to_y * 16 + mine_b, to_core), device_id_type=MESH,
        ).start()
    seven = in_a.at[pl.ds(0, 7)]
    pltpu.make_async_copy(seven, seven, mrecv_sem.at[0]).wait()
    for k in range(8):
        out_b[:, k, :] = in_a[k]
    in_b[mine_b] = out_b[mine_b]
    for k in range(1, 16):
        to = ((x + k // 4) % 4) * 4 + (z + k % 4) % 4
        pltpu.make_async_remote_copy(
            src_ref=out_b.at[to], dst_ref=in_b.at[mine_b], send_sem=nsend_sem, recv_sem=mrecv_sem.at[1],
            device_id=(y * 16 + to, core), device_id_type=MESH,
        ).start()
    fifteen = in_b.at[pl.ds(0, 15)]
    pltpu.make_async_copy(fifteen, fifteen, mrecv_sem.at[1]).wait()
    small_ref[16:144, :] = in_b[...].reshape(128, 128)

    drain(lists.at[pl.ds(0, 9)], list_sem)
    drain(lines.at[pl.ds(0, 9)], line_sem)
    drain(outb.at[pl.ds(0, 93)], send_sem)
    drain(out_a.at[pl.ds(0, 7)], msend_sem)
    drain(out_b.at[pl.ds(0, 15)], nsend_sem)
    expo_copy.wait()


def permuted(values, in_rows, out_rows, first, second):
    first[...] = jnp.concatenate([values.astype(F32), jnp.zeros((112, 128), F32)], axis=0).T
    for k in range(8):
        second[out_rows(k), :] = first[in_rows(k), :]
    return second[...].T[0:16].astype(I32)


def finish(small_ref, bld_ref, expo_in, level_ref, build_ref, expo_ref, passing, first, second, sems_in, sems_out):
    height = WIDTH // CUTS
    cuts = [pl.ds(k * height, height) for k in range(CUTS)]
    loads = [pltpu.make_async_copy(expo_in.at[c], passing.at[c], sems_in.at[k]) for k, c in enumerate(cuts)]
    stores = [pltpu.make_async_copy(passing.at[c], expo_ref.at[c], sems_out.at[k]) for k, c in enumerate(cuts)]
    for load in loads:
        load.start()
    for load, store in zip(loads, stores):
        load.wait()
        store.start()
    level_ref[...] = small_ref[0:16, :]
    got = small_ref[16:144, :].T
    bld = permuted(
        bld_ref[...], lambda k: pl.ds(k // 2 * 32 + k % 2, 16, stride=2), lambda k: pl.ds(k, 16, stride=8), first, second
    )
    bld_high, bld_low = bld // 128, bld % 128
    sub = lax.broadcasted_iota(I32, (128, 128), 0)
    lhs, hots = [], []
    for c in range(CAP_ADDR):
        mine = lax.broadcasted_iota(I32, (16, 128), 0) == bld_high[c : c + 1]
        spread = jnp.where(mine, got[c : c + 1], 0.0)
        count = jnp.where(mine, got[16 + c : 17 + c], 0.0)
        lhs.append(jnp.concatenate([*split3(spread), count.astype(BF16)], axis=0))
        hots.append(jnp.where(sub == bld_low[c : c + 1], 1.0, 0.0).astype(BF16))
    sums = lax.dot_general(
        jnp.concatenate(lhs, axis=1), jnp.concatenate(hots, axis=1), (((1,), (1,)), ((), ())), preferred_element_type=F32
    )
    build_ref[...] = (sums[0:16] + sums[16:32] + sums[32:48]) / jnp.maximum(sums[48:64], 1.0)
    for store in stores:
        store.wait()


def local(emission, path_sends, tile_slots, geometry, absorption, hour_period, dwellings, addr_sends, addr_building):
    vmem, hbm = pl.BlockSpec(memory_space=pltpu.VMEM), pl.BlockSpec(memory_space=pl.ANY)
    small, exposure = pl.pallas_call(
        kernel,
        out_shape=(
            jax.ShapeDtypeStruct((144, 128), F32),
            jax.ShapeDtypeStruct((WIDTH, TILE_DEV * RECV_TILE), F32),
        ),
        in_specs=[hbm] * 8,
        out_specs=(vmem, hbm),
        scratch_shapes=[
            pltpu.VMEM((CAP, DEVICES), I32),
            pltpu.VMEM((TILE_DEV, PATHS_TILE), I32),
            pltpu.VMEM((TILE_DEV, BANDS, PATHS_TILE), BF16),
            pltpu.SMEM((HOURS,), I32),
            pltpu.VMEM((16, 128), I32),
            pltpu.VMEM((CAP_ADDR, DEVICES), I32),
            pltpu.VMEM((WIDTH, TILE_DEV * RECV_TILE), F32),
            pltpu.VMEM((4, 4, 4, 1, 128), F32),
            pltpu.VMEM((4, 4, 4, 1, 128), F32),
            pltpu.VMEM((12, PART, SEG_DEV), BF16),
            pltpu.VMEM((12, 4, 4, 1, 128), F32),
            pltpu.VMEM((96, PART, 256), BF16),
            pltpu.VMEM((96, PART, 256), BF16),
            pltpu.VMEM((WIDTH, PATHS), F32),
            pltpu.VMEM((12, TILE_DEV, PATHS_TILE), I32),
            pltpu.VMEM((3, TILE_DEV, PATHS_TILE), I32),
            pltpu.VMEM((TILE_DEV, RECV_TILE, PATHS_TILE), BF16),
            pltpu.VMEM((WIDTH, 128), F32),
            pltpu.VMEM((128, 128), F32),
            pltpu.VMEM((128, 128), F32),
            pltpu.VMEM((128, 2048), BF16),
            pltpu.VMEM((8, 16, 128), F32),
            pltpu.VMEM((8, 16, 128), F32),
            pltpu.VMEM((16, 8, 128), F32),
            pltpu.VMEM((16, 8, 128), F32),
            pltpu.SemaphoreType.DMA((6,)),
            pltpu.SemaphoreType.DMA((3,)),
            pltpu.SemaphoreType.DMA,
            pltpu.SemaphoreType.DMA,
            pltpu.SemaphoreType.DMA,
            pltpu.SemaphoreType.DMA,
            pltpu.SemaphoreType.DMA,
            pltpu.SemaphoreType.DMA((3,)),
            pltpu.SemaphoreType.DMA((3,)),
            pltpu.SemaphoreType.DMA((12,)),
            pltpu.SemaphoreType.DMA,
            pltpu.SemaphoreType.DMA,
            pltpu.SemaphoreType.DMA((2,)),
        ],
        compiler_params=pltpu.CompilerParams(collective_id=0, has_side_effects=True, vmem_limit_bytes=60 * 2**20),
        name="noise_map",
    )(
        emission.T,
        path_sends[0].T,
        tile_slots,
        geometry,
        absorption,
        hour_period,
        dwellings.reshape(16, 128),
        addr_sends[0].T,
    )
    level, building, exposure = pl.pallas_call(
        finish,
        out_shape=(
            jax.ShapeDtypeStruct((16, 128), F32),
            jax.ShapeDtypeStruct((16, 128), F32),
            jax.ShapeDtypeStruct((WIDTH, TILE_DEV * RECV_TILE), F32),
        ),
        in_specs=[vmem, vmem, hbm],
        out_specs=(vmem, vmem, hbm),
        scratch_shapes=[
            pltpu.VMEM((WIDTH, TILE_DEV * RECV_TILE), F32),
            pltpu.VMEM((128, 128), F32),
            pltpu.VMEM((128, 128), F32),
            pltpu.SemaphoreType.DMA((CUTS,)),
            pltpu.SemaphoreType.DMA((CUTS,)),
        ],
        compiler_params=pltpu.CompilerParams(vmem_limit_bytes=60 * 2**20),
        name="buildings",
    )(small, addr_building[0].T, exposure)
    return level.reshape(-1), building.reshape(-1), exposure.T


def solution(mesh):
    both = ("region", "band")
    in_specs = (P(both, None), P(both, None, None), P(both, None), P(both, None, None), P(both, None, None), P(), P(both), P(both, None, None), P(both, None, None))
    out_specs = (P(both), P(both), P(both, None))
    return jax.shard_map(local, mesh=mesh, in_specs=in_specs, out_specs=out_specs, check_vma=False)
```

```python
import math

import jax
import jax.numpy as jnp
from jax import lax
from jax.experimental import pallas as pl
from jax.experimental.pallas import tpu as pltpu
from jax.sharding import PartitionSpec as P

BANDS = 8
HOURS = 24
WIDTH = BANDS * HOURS
SEG_DEV = 512
CAP = 64
TILE_DEV = 8
RECV_TILE = 256
PATHS_TILE = 512
CAP_ADDR = 16
DEVICES = 128
PATHS = TILE_DEV * PATHS_TILE
PART = 64
STRIDE = (16, 4, 1)
PLANE = ((1, 2), (0, 2), (0, 1))
SPAN = 4096
CUTS = 6
AHEAD = 7
A_WEIGHTING_DB = (-26.2, -16.1, -8.6, -3.2, 0.0, 1.2, 1.0, -1.1)
MESH = pl.DeviceIdType.MESH
BF16, F32, I32 = jnp.bfloat16, jnp.float32, jnp.int32


def split3(value):
    high = value.astype(BF16)
    rest = value - high.astype(F32)
    mid = rest.astype(BF16)
    return high, mid, (rest - mid.astype(F32)).astype(BF16)


def my_place():
    region, core = lax.axis_index("region"), lax.axis_index("band")
    return (region // 16, (region // 4) % 4, region % 4), core


def one_hot(row, count):
    lines = lax.broadcasted_iota(I32, (count, row.shape[1]), 0)
    return jnp.where(lines == row, 1.0, 0.0).astype(BF16)


def drain(ref, sem):
    pltpu.make_async_copy(ref, ref, sem).wait()


def kernel(
    em_hbm, ps_hbm, slot_hbm, geo_hbm, abs_hbm, hour_hbm, dwell_hbm, addr_hbm,
    small_ref, expo_hbm,
    ps_ref, slot_ref, abs_ref, hour_ref, dwell_ref, addr_ref, expo_ref, even, odd, lines, lists, outb, recv, acc, label, sender, geo, weight, first, second, hots, out_a, in_a, out_b, in_b,
    in_sem, own_sem, out_sem, geo_sem, line_sem, list_sem, send_sem, line_in, list_in, recv_sem, msend_sem, nsend_sem, mrecv_sem,
):
    at, core = my_place()
    y, x, z = at
    inputs = ((ps_hbm, ps_ref), (slot_hbm, slot_ref), (abs_hbm, abs_ref), (hour_hbm, hour_ref), (dwell_hbm, dwell_ref), (addr_hbm, addr_ref))
    inputs = [pltpu.make_async_copy(a, b, in_sem.at[k]) for k, (a, b) in enumerate(inputs)]
    for copy in inputs:
        copy.start()
    own_lines = [pltpu.make_async_copy(em_hbm.at[pl.ds(p * PART, PART)], lines.at[p * 4], own_sem.at[p]) for p in range(3)]
    for copy in own_lines:
        copy.start()
    geo_copy = pltpu.make_async_copy(geo_hbm, geo, geo_sem)
    geo_copy.start()
    barrier = pltpu.get_barrier_semaphore()
    peers = 0
    for dy in range(4):
        for dx in range(4):
            for dz in range(4):
                for dc in range(2):
                    if 0 in (dy, dx, dz) and (dy, dx, dz, dc) != (0, 0, 0, 0):
                        to = ((y + dy) % 4) * 16 + ((x + dx) % 4) * 4 + (z + dz) % 4
                        pl.semaphore_signal(barrier, inc=1, device_id=(to, (core + dc) % 2), device_id_type=MESH)
                        peers += 1

    inputs[0].wait()
    entries = ps_ref[...].astype(F32)
    first[...] = jnp.concatenate([entries, entries], axis=0).T
    zero, one = first[pl.ds(0, 64, stride=2), :], first[pl.ds(1, 64, stride=2), :]
    left = lax.broadcasted_iota(I32, (64, 128), 1) < 64
    both, swapped = jnp.where(left, zero, one), jnp.where(left, one, zero)
    for a in range(4):
        for b in range(4):
            cut = slice((a * 4 + b) * 4, (a * 4 + b) * 4 + 4)
            even[a, b, :, 0, :] = both[cut]
            odd[a, b, :, 0, :] = swapped[cut]

    pl.semaphore_wait(barrier, peers)

    def plane_of(ref, p, where):
        return ref.at[where] if p == 0 else ref.at[:, where] if p == 1 else ref.at[:, :, where]

    for j in (1, 3, 2):
        for p in range(3):
            where = (at[p] + j) % 4
            to = sum(STRIDE[q] * (where if q == p else at[q]) for q in range(3))
            pltpu.make_async_remote_copy(
                src_ref=plane_of(odd if j % 2 else even, p, where), dst_ref=lists.at[p * 4 + j],
                send_sem=list_sem, recv_sem=list_in.at[p], device_id=(to, core), device_id_type=MESH,
            ).start()
            pltpu.make_async_remote_copy(
                src_ref=em_hbm.at[pl.ds(p * PART, PART)], dst_ref=lines.at[p * 4 + j],
                send_sem=line_sem, recv_sem=line_in.at[p], device_id=(to, core), device_id_type=MESH,
            ).start()
    for p in range(3):
        lists[p * 4] = plane_of(even, p, at[p])[...]
        own_lines[p].wait()
    for copy in inputs[1:]:
        copy.wait()

    def pick(u, p):
        b1, b2 = PLANE[p]
        line1 = [(at[b1] + u + 4 - v) % 4 for v in range(4)]
        line2 = [(at[b2] + v) % 4 for v in range(4)]

        @pl.when(u == 0)
        def _():
            drain(lists.at[pl.ds(p * 4 + 1, 3)], list_in.at[p])
            drain(lines.at[pl.ds(p * 4 + 1, 3)], line_in.at[p])

        found = []
        for i in range(4):
            row = jnp.concatenate([lists[p * 4 + i, line1[v], line2[v]] for v in range(4)], axis=1)
            upper = row >= 256.0
            table = one_hot(jnp.where(upper, row - 256.0, row).astype(I32), 256)
            source = lines[p * 4 + i]
            halves = jnp.concatenate([source[:, 0:256], source[:, 256:512]], axis=0)
            out = jnp.dot(halves, table, preferred_element_type=F32)
            found.append(jnp.where(upper, out[PART:], out[:PART]))
        low = lax.broadcasted_iota(I32, (PART, 512), 1) % 128 < 64
        for k in range(2):
            pairs = []
            for i in (0, 2):
                a, b = (found[i], found[i + 1]) if k == 0 else (found[i + 1], found[i])
                pairs.append(jnp.where(low, a, b).astype(BF16))
            for v in range(4):
                cut = slice(v * 128, (v + 1) * 128)
                outb[(p * 4 + u) * 8 + k * 4 + v] = jnp.concatenate([pairs[0][:, cut], pairs[1][:, cut]], axis=1)
        for dc in range(2):
            to_core = (core + dc) % 2
            for v in range(4):
                to = STRIDE[p] * at[p] + STRIDE[b1] * line1[v] + STRIDE[b2] * line2[v]
                copy = pltpu.make_async_remote_copy(
                    src_ref=outb.at[(p * 4 + u) * 8 + to_core * 4 + v], dst_ref=recv.at[(p * 4 + u) * 8 + dc * 4 + v],
                    send_sem=send_sem, recv_sem=recv_sem.at[p * 4 + u], device_id=(to, to_core), device_id_type=MESH,
                )
                if dc or v:
                    copy.start()
                else:

                    @pl.when(u > 0)
                    def _():
                        copy.start()

                    @pl.when(u == 0)
                    def _():
                        recv[p * 32] = outb[p * 32 + core * 4]

    slots = slot_ref[...]
    safe = jnp.maximum(slots, 0)
    source, entry = safe // CAP, safe % CAP
    apart = (
        (y + 4 - source // 32) % 4, (x + 4 - (source // 8) % 4) % 4, (z + 4 - (source // 2) % 4) % 4,
    )
    other = (core + 2 - source % 2) % 2
    for p in range(3):
        b1, b2 = PLANE[p]
        lane = (apart[p] // 2) * 128 + ((apart[p] + core) % 2) * 64 + entry
        group = jnp.where(slots >= 0, (apart[b1] + apart[b2]) % 4, -1)
        for g in range(4):
            label[p * 4 + g] = jnp.where(group == g, lane, -1)
        sender[p] = other * 4 + apart[b2]

    r = lax.broadcasted_iota(I32, (WIDTH, 128), 0)
    scale = jnp.zeros((WIDTH, 128), F32)
    for b in range(BANDS):
        scale = jnp.where(r // HOURS == b, jnp.float32(10.0 ** (A_WEIGHTING_DB[b] / 10.0)), scale)
    gain = jnp.zeros((WIDTH, 128), F32)
    for h in range(HOURS):
        period = hour_ref[h]
        g = jnp.where(period == 0, 1.0, jnp.where(period == 1, jnp.float32(10.0**0.5), jnp.where(period == 2, 10.0, 0.0)))
        gain = jnp.where(r % HOURS == h, g.astype(F32), gain)
    weight[...] = scale * gain / HOURS

    addr = permuted(
        addr_ref[...], lambda k: pl.ds(k // 2 * 32 + k % 2, 16, stride=2), lambda k: pl.ds(k * 16, 16), first, second
    )
    addr_high = jnp.maximum(addr, 0) // 128
    addr_low = jnp.where(addr >= 0, addr % 128, -1)
    for c in range(CAP_ADDR):
        hots[:, c * 128 : (c + 1) * 128] = one_hot(addr_low[c : c + 1], 128)
    acc[...] = jnp.zeros_like(acc)

    def gather(u, p):
        step = p * 4 + u

        @pl.when(u == 0)
        def _():
            drain(recv.at[pl.ds(p * 32 + 1, 7)], recv_sem.at[step])

        @pl.when(u > 0)
        def _():
            drain(recv.at[pl.ds(step * 8, 8)], recv_sem.at[step])

        def some_paths(n, inner):
            def row_of(ref, index):
                first_tile = n * (SPAN // PATHS_TILE)
                return jnp.concatenate([ref[index, pl.ds(first_tile + m, 1), :] for m in range(SPAN // PATHS_TILE)], axis=1)

            table = one_hot(row_of(label, step), 256)
            data = recv[pl.ds(step * 8, 8)].reshape(8 * PART, 256)
            out = jnp.dot(data, table, preferred_element_type=F32)
            which = row_of(sender, p)
            mine = out[0:PART]
            for k in range(1, 8):
                mine = jnp.where(which == k, out[k * PART : (k + 1) * PART], mine)
            cut = (slice(p * PART, (p + 1) * PART), pl.ds(pl.multiple_of(n * SPAN, SPAN), SPAN))
            acc[cut] = acc[cut] + mine
            return inner

        lax.fori_loop(0, PATHS // SPAN, some_paths, 0)

    def turn(u, carry):
        for p in range(3):

            @pl.when(u < 4)
            def _():
                pick(u, p)

            late = (p - AHEAD) % 3
            back = (AHEAD + late - p) // 3

            @pl.when((u >= back) & (u < 4 + back))
            def _():
                gather(u - back, late)

        return carry

    lax.fori_loop(0, 4 + (AHEAD + 2) // 3, turn, 0)
    geo_copy.wait()

    def tile(t, carry):
        gathered = acc[:, pl.ds(pl.multiple_of(t * PATHS_TILE, PATHS_TILE), PATHS_TILE)]
        damp = abs_ref[t].astype(F32)
        factor = jnp.concatenate(
            [jnp.broadcast_to(damp[b : b + 1], (HOURS, PATHS_TILE)) for b in range(BANDS)], axis=0
        )
        mixed = (factor * gathered).astype(BF16)
        exposure = lax.dot_general(mixed, geo[t], (((1,), (1,)), ((), ())), preferred_element_type=F32)
        expo_ref[:, pl.ds(pl.multiple_of(t * RECV_TILE, RECV_TILE), RECV_TILE)] = exposure
        for half in range(2):
            energy = jnp.sum(exposure[:, half * 128 : (half + 1) * 128] * weight[...], axis=0, keepdims=True)
            small_ref[pl.ds(2 * t + half, 1), :] = jnp.log(energy) * jnp.float32(1.0 / math.log(10.0))
        return carry

    lax.fori_loop(0, TILE_DEV, tile, 0, unroll=4)

    expo_copy = pltpu.make_async_copy(expo_ref, expo_hbm, out_sem)
    expo_copy.start()
    dwell = dwell_ref[...].astype(F32)
    table = jnp.concatenate([*split3(dwell * small_ref[0:16, :]), dwell.astype(BF16)], axis=0)
    found = jnp.dot(table, hots[...], preferred_element_type=F32)
    level_rows = found[0:16] + found[16:32] + found[32:48]
    weighted, dwelt = [], []
    for c in range(CAP_ADDR):
        lanes = slice(c * 128, (c + 1) * 128)
        mine = lax.broadcasted_iota(I32, (16, 128), 0) == addr_high[c : c + 1]
        weighted.append(jnp.sum(jnp.where(mine, level_rows[:, lanes], 0.0), axis=0, keepdims=True))
        dwelt.append(jnp.sum(jnp.where(mine, found[48:64, lanes], 0.0), axis=0, keepdims=True))
    out_a[...] = jnp.concatenate(weighted + dwelt + [jnp.zeros((96, 128), F32)], axis=0).T.reshape(8, 16, 128)
    mine_a, mine_b = y * 2 + core, x * 4 + z
    in_a[mine_a] = out_a[mine_a]
    for k in range(1, 8):
        to_y, to_core = (y + k // 2) % 4, (core + k % 2) % 2
        pltpu.make_async_remote_copy(
            src_ref=out_a.at[to_y * 2 + to_core], dst_ref=in_a.at[mine_a], send_sem=msend_sem, recv_sem=mrecv_sem.at[0],
            device_id=(to_y * 16 + mine_b, to_core), device_id_type=MESH,
        ).start()
    seven = in_a.at[pl.ds(0, 7)]
    pltpu.make_async_copy(seven, seven, mrecv_sem.at[0]).wait()
    for k in range(8):
        out_b[:, k, :] = in_a[k]
    in_b[mine_b] = out_b[mine_b]
    for k in range(1, 16):
        to = ((x + k // 4) % 4) * 4 + (z + k % 4) % 4
        pltpu.make_async_remote_copy(
            src_ref=out_b.at[to], dst_ref=in_b.at[mine_b], send_sem=nsend_sem, recv_sem=mrecv_sem.at[1],
            device_id=(y * 16 + to, core), device_id_type=MESH,
        ).start()
    fifteen = in_b.at[pl.ds(0, 15)]
    pltpu.make_async_copy(fifteen, fifteen, mrecv_sem.at[1]).wait()
    small_ref[16:144, :] = in_b[...].reshape(128, 128)

    drain(lists.at[pl.ds(0, 9)], list_sem)
    drain(lines.at[pl.ds(0, 9)], line_sem)
    drain(outb.at[pl.ds(0, 93)], send_sem)
    drain(out_a.at[pl.ds(0, 7)], msend_sem)
    drain(out_b.at[pl.ds(0, 15)], nsend_sem)
    expo_copy.wait()


def permuted(values, in_rows, out_rows, first, second):
    first[...] = jnp.concatenate([values.astype(F32), jnp.zeros((112, 128), F32)], axis=0).T
    for k in range(8):
        second[out_rows(k), :] = first[in_rows(k), :]
    return second[...].T[0:16].astype(I32)


def finish(small_ref, bld_ref, expo_in, level_ref, build_ref, expo_ref, passing, first, second, sems_in, sems_out):
    height = WIDTH // CUTS
    cuts = [pl.ds(k * height, height) for k in range(CUTS)]
    loads = [pltpu.make_async_copy(expo_in.at[c], passing.at[c], sems_in.at[k]) for k, c in enumerate(cuts)]
    stores = [pltpu.make_async_copy(passing.at[c], expo_ref.at[c], sems_out.at[k]) for k, c in enumerate(cuts)]
    for load in loads:
        load.start()
    for load, store in zip(loads, stores):
        load.wait()
        store.start()
    level_ref[...] = small_ref[0:16, :]
    got = small_ref[16:144, :].T
    bld = permuted(
        bld_ref[...], lambda k: pl.ds(k // 2 * 32 + k % 2, 16, stride=2), lambda k: pl.ds(k, 16, stride=8), first, second
    )
    bld_high, bld_low = bld // 128, bld % 128
    sub = lax.broadcasted_iota(I32, (128, 128), 0)
    lhs, hots = [], []
    for c in range(CAP_ADDR):
        mine = lax.broadcasted_iota(I32, (16, 128), 0) == bld_high[c : c + 1]
        spread = jnp.where(mine, got[c : c + 1], 0.0)
        count = jnp.where(mine, got[16 + c : 17 + c], 0.0)
        lhs.append(jnp.concatenate([*split3(spread), count.astype(BF16)], axis=0))
        hots.append(jnp.where(sub == bld_low[c : c + 1], 1.0, 0.0).astype(BF16))
    sums = lax.dot_general(
        jnp.concatenate(lhs, axis=1), jnp.concatenate(hots, axis=1), (((1,), (1,)), ((), ())), preferred_element_type=F32
    )
    build_ref[...] = (sums[0:16] + sums[16:32] + sums[32:48]) / jnp.maximum(sums[48:64], 1.0)
    for store in stores:
        store.wait()


def local(emission, path_sends, tile_slots, geometry, absorption, hour_period, dwellings, addr_sends, addr_building):
    vmem, hbm = pl.BlockSpec(memory_space=pltpu.VMEM), pl.BlockSpec(memory_space=pl.ANY)
    small, exposure = pl.pallas_call(
        kernel,
        out_shape=(
            jax.ShapeDtypeStruct((144, 128), F32),
            jax.ShapeDtypeStruct((WIDTH, TILE_DEV * RECV_TILE), F32),
        ),
        in_specs=[hbm] * 8,
        out_specs=(vmem, hbm),
        scratch_shapes=[
            pltpu.VMEM((CAP, DEVICES), I32),
            pltpu.VMEM((TILE_DEV, PATHS_TILE), I32),
            pltpu.VMEM((TILE_DEV, BANDS, PATHS_TILE), BF16),
            pltpu.SMEM((HOURS,), I32),
            pltpu.VMEM((16, 128), I32),
            pltpu.VMEM((CAP_ADDR, DEVICES), I32),
            pltpu.VMEM((WIDTH, TILE_DEV * RECV_TILE), F32),
            pltpu.VMEM((4, 4, 4, 1, 128), F32),
            pltpu.VMEM((4, 4, 4, 1, 128), F32),
            pltpu.VMEM((12, PART, SEG_DEV), BF16),
            pltpu.VMEM((12, 4, 4, 1, 128), F32),
            pltpu.VMEM((96, PART, 256), BF16),
            pltpu.VMEM((96, PART, 256), BF16),
            pltpu.VMEM((WIDTH, PATHS), F32),
            pltpu.VMEM((12, TILE_DEV, PATHS_TILE), I32),
            pltpu.VMEM((3, TILE_DEV, PATHS_TILE), I32),
            pltpu.VMEM((TILE_DEV, RECV_TILE, PATHS_TILE), BF16),
            pltpu.VMEM((WIDTH, 128), F32),
            pltpu.VMEM((128, 128), F32),
            pltpu.VMEM((128, 128), F32),
            pltpu.VMEM((128, 2048), BF16),
            pltpu.VMEM((8, 16, 128), F32),
            pltpu.VMEM((8, 16, 128), F32),
            pltpu.VMEM((16, 8, 128), F32),
            pltpu.VMEM((16, 8, 128), F32),
            pltpu.SemaphoreType.DMA((6,)),
            pltpu.SemaphoreType.DMA((3,)),
            pltpu.SemaphoreType.DMA,
            pltpu.SemaphoreType.DMA,
            pltpu.SemaphoreType.DMA,
            pltpu.SemaphoreType.DMA,
            pltpu.SemaphoreType.DMA,
            pltpu.SemaphoreType.DMA((3,)),
            pltpu.SemaphoreType.DMA((3,)),
            pltpu.SemaphoreType.DMA((12,)),
            pltpu.SemaphoreType.DMA,
            pltpu.SemaphoreType.DMA,
            pltpu.SemaphoreType.DMA((2,)),
        ],
        compiler_params=pltpu.CompilerParams(collective_id=0, has_side_effects=True, vmem_limit_bytes=60 * 2**20),
        name="noise_map",
    )(
        emission.T,
        path_sends[0].T,
        tile_slots,
        geometry,
        absorption,
        hour_period,
        dwellings.reshape(16, 128),
        addr_sends[0].T,
    )
    level, building, exposure = pl.pallas_call(
        finish,
        out_shape=(
            jax.ShapeDtypeStruct((16, 128), F32),
            jax.ShapeDtypeStruct((16, 128), F32),
            jax.ShapeDtypeStruct((WIDTH, TILE_DEV * RECV_TILE), F32),
        ),
        in_specs=[vmem, vmem, hbm],
        out_specs=(vmem, vmem, hbm),
        scratch_shapes=[
            pltpu.VMEM((WIDTH, TILE_DEV * RECV_TILE), F32),
            pltpu.VMEM((128, 128), F32),
            pltpu.VMEM((128, 128), F32),
            pltpu.SemaphoreType.DMA((CUTS,)),
            pltpu.SemaphoreType.DMA((CUTS,)),
        ],
        compiler_params=pltpu.CompilerParams(vmem_limit_bytes=60 * 2**20),
        name="buildings",
    )(small, addr_building[0].T, exposure)
    return level.reshape(-1), building.reshape(-1), exposure.T


def solution(mesh):
    both = ("region", "band")
    in_specs = (P(both, None), P(both, None, None), P(both, None), P(both, None, None), P(both, None, None), P(), P(both), P(both, None, None), P(both, None, None))
    out_specs = (P(both), P(both), P(both, None))
    return jax.shard_map(local, mesh=mesh, in_specs=in_specs, out_specs=out_specs, check_vma=False)
```

```python
import math

import jax
import jax.numpy as jnp
from jax import lax
from jax.experimental import pallas as pl
from jax.experimental.pallas import tpu as pltpu
from jax.sharding import PartitionSpec as P

BANDS = 8
HOURS = 24
WIDTH = BANDS * HOURS
SEG_DEV = 512
CAP = 64
TILE_DEV = 8
RECV_TILE = 256
PATHS_TILE = 512
CAP_ADDR = 16
DEVICES = 128
PATHS = TILE_DEV * PATHS_TILE
PART = 64
STRIDE = (16, 4, 1)
PLANE = ((1, 2), (0, 2), (0, 1))
SPAN = 4096
CUTS = 3
AHEAD = 7
A_WEIGHTING_DB = (-26.2, -16.1, -8.6, -3.2, 0.0, 1.2, 1.0, -1.1)
MESH = pl.DeviceIdType.MESH
BF16, F32, I32 = jnp.bfloat16, jnp.float32, jnp.int32


def split3(value):
    high = value.astype(BF16)
    rest = value - high.astype(F32)
    mid = rest.astype(BF16)
    return high, mid, (rest - mid.astype(F32)).astype(BF16)


def my_place():
    region, core = lax.axis_index("region"), lax.axis_index("band")
    return (region // 16, (region // 4) % 4, region % 4), core


def one_hot(row, count):
    lines = lax.broadcasted_iota(I32, (count, row.shape[1]), 0)
    return jnp.where(lines == row, 1.0, 0.0).astype(BF16)


def drain(ref, sem):
    pltpu.make_async_copy(ref, ref, sem).wait()


def kernel(
    em_hbm, ps_hbm, slot_hbm, geo_hbm, abs_hbm, hour_hbm, dwell_hbm, addr_hbm,
    small_ref, expo_hbm,
    ps_ref, slot_ref, abs_ref, hour_ref, dwell_ref, addr_ref, expo_ref, even, odd, lines, lists, outb, recv, acc, label, sender, geo, weight, first, second, hots, out_a, in_a, out_b, in_b,
    in_sem, own_sem, out_sem, geo_sem, line_sem, list_sem, send_sem, line_in, list_in, recv_sem, msend_sem, nsend_sem, mrecv_sem,
):
    at, core = my_place()
    y, x, z = at
    inputs = ((ps_hbm, ps_ref), (slot_hbm, slot_ref), (abs_hbm, abs_ref), (hour_hbm, hour_ref), (dwell_hbm, dwell_ref), (addr_hbm, addr_ref))
    inputs = [pltpu.make_async_copy(a, b, in_sem.at[k]) for k, (a, b) in enumerate(inputs)]
    for copy in inputs:
        copy.start()
    own_lines = [pltpu.make_async_copy(em_hbm.at[pl.ds(p * PART, PART)], lines.at[p * 4], own_sem.at[p]) for p in range(3)]
    for copy in own_lines:
        copy.start()
    geo_copy = pltpu.make_async_copy(geo_hbm, geo, geo_sem)
    geo_copy.start()
    barrier = pltpu.get_barrier_semaphore()
    peers = 0
    for dy in range(4):
        for dx in range(4):
            for dz in range(4):
                for dc in range(2):
                    if 0 in (dy, dx, dz) and (dy, dx, dz, dc) != (0, 0, 0, 0):
                        to = ((y + dy) % 4) * 16 + ((x + dx) % 4) * 4 + (z + dz) % 4
                        pl.semaphore_signal(barrier, inc=1, device_id=(to, (core + dc) % 2), device_id_type=MESH)
                        peers += 1

    inputs[0].wait()
    entries = ps_ref[...].astype(F32)
    first[...] = jnp.concatenate([entries, entries], axis=0).T
    zero, one = first[pl.ds(0, 64, stride=2), :], first[pl.ds(1, 64, stride=2), :]
    left = lax.broadcasted_iota(I32, (64, 128), 1) < 64
    both, swapped = jnp.where(left, zero, one), jnp.where(left, one, zero)
    for a in range(4):
        for b in range(4):
            cut = slice((a * 4 + b) * 4, (a * 4 + b) * 4 + 4)
            even[a, b, :, 0, :] = both[cut]
            odd[a, b, :, 0, :] = swapped[cut]

    pl.semaphore_wait(barrier, peers)

    def plane_of(ref, p, where):
        return ref.at[where] if p == 0 else ref.at[:, where] if p == 1 else ref.at[:, :, where]

    for j in (1, 3, 2):
        for p in range(3):
            where = (at[p] + j) % 4
            to = sum(STRIDE[q] * (where if q == p else at[q]) for q in range(3))
            pltpu.make_async_remote_copy(
                src_ref=plane_of(odd if j % 2 else even, p, where), dst_ref=lists.at[p * 4 + j],
                send_sem=list_sem, recv_sem=list_in.at[p], device_id=(to, core), device_id_type=MESH,
            ).start()
            pltpu.make_async_remote_copy(
                src_ref=em_hbm.at[pl.ds(p * PART, PART)], dst_ref=lines.at[p * 4 + j],
                send_sem=line_sem, recv_sem=line_in.at[p], device_id=(to, core), device_id_type=MESH,
            ).start()
    for p in range(3):
        lists[p * 4] = plane_of(even, p, at[p])[...]
        own_lines[p].wait()
    for copy in inputs[1:]:
        copy.wait()

    def pick(u, p):
        b1, b2 = PLANE[p]
        line1 = [(at[b1] + u + 4 - v) % 4 for v in range(4)]
        line2 = [(at[b2] + v) % 4 for v in range(4)]

        @pl.when(u == 0)
        def _():
            drain(lists.at[pl.ds(p * 4 + 1, 3)], list_in.at[p])
            drain(lines.at[pl.ds(p * 4 + 1, 3)], line_in.at[p])

        found = []
        for i in range(4):
            row = jnp.concatenate([lists[p * 4 + i, line1[v], line2[v]] for v in range(4)], axis=1)
            upper = row >= 256.0
            table = one_hot(jnp.where(upper, row - 256.0, row).astype(I32), 256)
            source = lines[p * 4 + i]
            halves = jnp.concatenate([source[:, 0:256], source[:, 256:512]], axis=0)
            out = jnp.dot(halves, table, preferred_element_type=F32)
            found.append(jnp.where(upper, out[PART:], out[:PART]))
        low = lax.broadcasted_iota(I32, (PART, 512), 1) % 128 < 64
        for k in range(2):
            pairs = []
            for i in (0, 2):
                a, b = (found[i], found[i + 1]) if k == 0 else (found[i + 1], found[i])
                pairs.append(jnp.where(low, a, b).astype(BF16))
            for v in range(4):
                cut = slice(v * 128, (v + 1) * 128)
                outb[(p * 4 + u) * 8 + k * 4 + v] = jnp.concatenate([pairs[0][:, cut], pairs[1][:, cut]], axis=1)
        for dc in range(2):
            to_core = (core + dc) % 2
            for v in range(4):
                to = STRIDE[p] * at[p] + STRIDE[b1] * line1[v] + STRIDE[b2] * line2[v]
                copy = pltpu.make_async_remote_copy(
                    src_ref=outb.at[(p * 4 + u) * 8 + to_core * 4 + v], dst_ref=recv.at[(p * 4 + u) * 8 + dc * 4 + v],
                    send_sem=send_sem, recv_sem=recv_sem.at[p * 4 + u], device_id=(to, to_core), device_id_type=MESH,
                )
                if dc or v:
                    copy.start()
                else:

                    @pl.when(u > 0)
                    def _():
                        copy.start()

                    @pl.when(u == 0)
                    def _():
                        recv[p * 32] = outb[p * 32 + core * 4]

    slots = slot_ref[...]
    safe = jnp.maximum(slots, 0)
    source, entry = safe // CAP, safe % CAP
    apart = (
        (y + 4 - source // 32) % 4, (x + 4 - (source // 8) % 4) % 4, (z + 4 - (source // 2) % 4) % 4,
    )
    other = (core + 2 - source % 2) % 2
    for p in range(3):
        b1, b2 = PLANE[p]
        lane = (apart[p] // 2) * 128 + ((apart[p] + core) % 2) * 64 + entry
        group = jnp.where(slots >= 0, (apart[b1] + apart[b2]) % 4, -1)
        for g in range(4):
            label[p * 4 + g] = jnp.where(group == g, lane, -1)
        sender[p] = other * 4 + apart[b2]

    r = lax.broadcasted_iota(I32, (WIDTH, 128), 0)
    scale = jnp.zeros((WIDTH, 128), F32)
    for b in range(BANDS):
        scale = jnp.where(r // HOURS == b, jnp.float32(10.0 ** (A_WEIGHTING_DB[b] / 10.0)), scale)
    gain = jnp.zeros((WIDTH, 128), F32)
    for h in range(HOURS):
        period = hour_ref[h]
        g = jnp.where(period == 0, 1.0, jnp.where(period == 1, jnp.float32(10.0**0.5), jnp.where(period == 2, 10.0, 0.0)))
        gain = jnp.where(r % HOURS == h, g.astype(F32), gain)
    weight[...] = scale * gain / HOURS

    addr = permuted(
        addr_ref[...], lambda k: pl.ds(k // 2 * 32 + k % 2, 16, stride=2), lambda k: pl.ds(k * 16, 16), first, second
    )
    addr_high = jnp.maximum(addr, 0) // 128
    addr_low = jnp.where(addr >= 0, addr % 128, -1)
    for c in range(CAP_ADDR):
        hots[:, c * 128 : (c + 1) * 128] = one_hot(addr_low[c : c + 1], 128)
    acc[...] = jnp.zeros_like(acc)

    def gather(u, p):
        step = p * 4 + u

        @pl.when(u == 0)
        def _():
            drain(recv.at[pl.ds(p * 32 + 1, 7)], recv_sem.at[step])

        @pl.when(u > 0)
        def _():
            drain(recv.at[pl.ds(step * 8, 8)], recv_sem.at[step])

        def some_paths(n, inner):
            def row_of(ref, index):
                first_tile = n * (SPAN // PATHS_TILE)
                return jnp.concatenate([ref[index, pl.ds(first_tile + m, 1), :] for m in range(SPAN // PATHS_TILE)], axis=1)

            table = one_hot(row_of(label, step), 256)
            data = recv[pl.ds(step * 8, 8)].reshape(8 * PART, 256)
            out = jnp.dot(data, table, preferred_element_type=F32)
            which = row_of(sender, p)
            mine = out[0:PART]
            for k in range(1, 8):
                mine = jnp.where(which == k, out[k * PART : (k + 1) * PART], mine)
            cut = (slice(p * PART, (p + 1) * PART), pl.ds(pl.multiple_of(n * SPAN, SPAN), SPAN))
            acc[cut] = acc[cut] + mine
            return inner

        lax.fori_loop(0, PATHS // SPAN, some_paths, 0)

    def turn(u, carry):
        for p in range(3):

            @pl.when(u < 4)
            def _():
                pick(u, p)

            late = (p - AHEAD) % 3
            back = (AHEAD + late - p) // 3

            @pl.when((u >= back) & (u < 4 + back))
            def _():
                gather(u - back, late)

        return carry

    lax.fori_loop(0, 4 + (AHEAD + 2) // 3, turn, 0)
    geo_copy.wait()

    def tile(t, carry):
        gathered = acc[:, pl.ds(pl.multiple_of(t * PATHS_TILE, PATHS_TILE), PATHS_TILE)]
        damp = abs_ref[t].astype(F32)
        factor = jnp.concatenate(
            [jnp.broadcast_to(damp[b : b + 1], (HOURS, PATHS_TILE)) for b in range(BANDS)], axis=0
        )
        mixed = (factor * gathered).astype(BF16)
        exposure = lax.dot_general(mixed, geo[t], (((1,), (1,)), ((), ())), preferred_element_type=F32)
        expo_ref[:, pl.ds(pl.multiple_of(t * RECV_TILE, RECV_TILE), RECV_TILE)] = exposure
        for half in range(2):
            energy = jnp.sum(exposure[:, half * 128 : (half + 1) * 128] * weight[...], axis=0, keepdims=True)
            small_ref[pl.ds(2 * t + half, 1), :] = jnp.log(energy) * jnp.float32(1.0 / math.log(10.0))
        return carry

    lax.fori_loop(0, TILE_DEV, tile, 0, unroll=8)

    expo_copy = pltpu.make_async_copy(expo_ref, expo_hbm, out_sem)
    expo_copy.start()
    dwell = dwell_ref[...].astype(F32)
    table = jnp.concatenate([*split3(dwell * small_ref[0:16, :]), dwell.astype(BF16)], axis=0)
    found = jnp.dot(table, hots[...], preferred_element_type=F32)
    level_rows = found[0:16] + found[16:32] + found[32:48]
    weighted, dwelt = [], []
    for c in range(CAP_ADDR):
        lanes = slice(c * 128, (c + 1) * 128)
        mine = lax.broadcasted_iota(I32, (16, 128), 0) == addr_high[c : c + 1]
        weighted.append(jnp.sum(jnp.where(mine, level_rows[:, lanes], 0.0), axis=0, keepdims=True))
        dwelt.append(jnp.sum(jnp.where(mine, found[48:64, lanes], 0.0), axis=0, keepdims=True))
    out_a[...] = jnp.concatenate(weighted + dwelt + [jnp.zeros((96, 128), F32)], axis=0).T.reshape(8, 16, 128)
    mine_a, mine_b = y * 2 + core, x * 4 + z
    in_a[mine_a] = out_a[mine_a]
    for k in range(1, 8):
        to_y, to_core = (y + k // 2) % 4, (core + k % 2) % 2
        pltpu.make_async_remote_copy(
            src_ref=out_a.at[to_y * 2 + to_core], dst_ref=in_a.at[mine_a], send_sem=msend_sem, recv_sem=mrecv_sem.at[0],
            device_id=(to_y * 16 + mine_b, to_core), device_id_type=MESH,
        ).start()
    seven = in_a.at[pl.ds(0, 7)]
    pltpu.make_async_copy(seven, seven, mrecv_sem.at[0]).wait()
    for k in range(8):
        out_b[:, k, :] = in_a[k]
    in_b[mine_b] = out_b[mine_b]
    for k in range(1, 16):
        to = ((x + k // 4) % 4) * 4 + (z + k % 4) % 4
        pltpu.make_async_remote_copy(
            src_ref=out_b.at[to], dst_ref=in_b.at[mine_b], send_sem=nsend_sem, recv_sem=mrecv_sem.at[1],
            device_id=(y * 16 + to, core), device_id_type=MESH,
        ).start()
    fifteen = in_b.at[pl.ds(0, 15)]
    pltpu.make_async_copy(fifteen, fifteen, mrecv_sem.at[1]).wait()
    small_ref[16:144, :] = in_b[...].reshape(128, 128)

    drain(lists.at[pl.ds(0, 9)], list_sem)
    drain(lines.at[pl.ds(0, 9)], line_sem)
    drain(outb.at[pl.ds(0, 93)], send_sem)
    drain(out_a.at[pl.ds(0, 7)], msend_sem)
    drain(out_b.at[pl.ds(0, 15)], nsend_sem)
    expo_copy.wait()


def permuted(values, in_rows, out_rows, first, second):
    first[...] = jnp.concatenate([values.astype(F32), jnp.zeros((112, 128), F32)], axis=0).T
    for k in range(8):
        second[out_rows(k), :] = first[in_rows(k), :]
    return second[...].T[0:16].astype(I32)


def finish(small_ref, bld_ref, expo_in, level_ref, build_ref, expo_ref, passing, first, second, sems_in, sems_out):
    height = WIDTH // CUTS
    cuts = [pl.ds(k * height, height) for k in range(CUTS)]
    loads = [pltpu.make_async_copy(expo_in.at[c], passing.at[c], sems_in.at[k]) for k, c in enumerate(cuts)]
    stores = [pltpu.make_async_copy(passing.at[c], expo_ref.at[c], sems_out.at[k]) for k, c in enumerate(cuts)]
    for load in loads:
        load.start()
    for load, store in zip(loads, stores):
        load.wait()
        store.start()
    level_ref[...] = small_ref[0:16, :]
    got = small_ref[16:144, :].T
    bld = permuted(
        bld_ref[...], lambda k: pl.ds(k // 2 * 32 + k % 2, 16, stride=2), lambda k: pl.ds(k, 16, stride=8), first, second
    )
    bld_high, bld_low = bld // 128, bld % 128
    sub = lax.broadcasted_iota(I32, (128, 128), 0)
    lhs, hots = [], []
    for c in range(CAP_ADDR):
        mine = lax.broadcasted_iota(I32, (16, 128), 0) == bld_high[c : c + 1]
        spread = jnp.where(mine, got[c : c + 1], 0.0)
        count = jnp.where(mine, got[16 + c : 17 + c], 0.0)
        lhs.append(jnp.concatenate([*split3(spread), count.astype(BF16)], axis=0))
        hots.append(jnp.where(sub == bld_low[c : c + 1], 1.0, 0.0).astype(BF16))
    sums = lax.dot_general(
        jnp.concatenate(lhs, axis=1), jnp.concatenate(hots, axis=1), (((1,), (1,)), ((), ())), preferred_element_type=F32
    )
    build_ref[...] = (sums[0:16] + sums[16:32] + sums[32:48]) / jnp.maximum(sums[48:64], 1.0)
    for store in stores:
        store.wait()


def local(emission, path_sends, tile_slots, geometry, absorption, hour_period, dwellings, addr_sends, addr_building):
    vmem, hbm = pl.BlockSpec(memory_space=pltpu.VMEM), pl.BlockSpec(memory_space=pl.ANY)
    small, exposure = pl.pallas_call(
        kernel,
        out_shape=(
            jax.ShapeDtypeStruct((144, 128), F32),
            jax.ShapeDtypeStruct((WIDTH, TILE_DEV * RECV_TILE), F32),
        ),
        in_specs=[hbm] * 8,
        out_specs=(vmem, hbm),
        scratch_shapes=[
            pltpu.VMEM((CAP, DEVICES), I32),
            pltpu.VMEM((TILE_DEV, PATHS_TILE), I32),
            pltpu.VMEM((TILE_DEV, BANDS, PATHS_TILE), BF16),
            pltpu.SMEM((HOURS,), I32),
            pltpu.VMEM((16, 128), I32),
            pltpu.VMEM((CAP_ADDR, DEVICES), I32),
            pltpu.VMEM((WIDTH, TILE_DEV * RECV_TILE), F32),
            pltpu.VMEM((4, 4, 4, 1, 128), F32),
            pltpu.VMEM((4, 4, 4, 1, 128), F32),
            pltpu.VMEM((12, PART, SEG_DEV), BF16),
            pltpu.VMEM((12, 4, 4, 1, 128), F32),
            pltpu.VMEM((96, PART, 256), BF16),
            pltpu.VMEM((96, PART, 256), BF16),
            pltpu.VMEM((WIDTH, PATHS), F32),
            pltpu.VMEM((12, TILE_DEV, PATHS_TILE), I32),
            pltpu.VMEM((3, TILE_DEV, PATHS_TILE), I32),
            pltpu.VMEM((TILE_DEV, RECV_TILE, PATHS_TILE), BF16),
            pltpu.VMEM((WIDTH, 128), F32),
            pltpu.VMEM((128, 128), F32),
            pltpu.VMEM((128, 128), F32),
            pltpu.VMEM((128, 2048), BF16),
            pltpu.VMEM((8, 16, 128), F32),
            pltpu.VMEM((8, 16, 128), F32),
            pltpu.VMEM((16, 8, 128), F32),
            pltpu.VMEM((16, 8, 128), F32),
            pltpu.SemaphoreType.DMA((6,)),
            pltpu.SemaphoreType.DMA((3,)),
            pltpu.SemaphoreType.DMA,
            pltpu.SemaphoreType.DMA,
            pltpu.SemaphoreType.DMA,
            pltpu.SemaphoreType.DMA,
            pltpu.SemaphoreType.DMA,
            pltpu.SemaphoreType.DMA((3,)),
            pltpu.SemaphoreType.DMA((3,)),
            pltpu.SemaphoreType.DMA((12,)),
            pltpu.SemaphoreType.DMA,
            pltpu.SemaphoreType.DMA,
            pltpu.SemaphoreType.DMA((2,)),
        ],
        compiler_params=pltpu.CompilerParams(collective_id=0, has_side_effects=True, vmem_limit_bytes=60 * 2**20),
        name="noise_map",
    )(
        emission.T,
        path_sends[0].T,
        tile_slots,
        geometry,
        absorption,
        hour_period,
        dwellings.reshape(16, 128),
        addr_sends[0].T,
    )
    level, building, exposure = pl.pallas_call(
        finish,
        out_shape=(
            jax.ShapeDtypeStruct((16, 128), F32),
            jax.ShapeDtypeStruct((16, 128), F32),
            jax.ShapeDtypeStruct((WIDTH, TILE_DEV * RECV_TILE), F32),
        ),
        in_specs=[vmem, vmem, hbm],
        out_specs=(vmem, vmem, hbm),
        scratch_shapes=[
            pltpu.VMEM((WIDTH, TILE_DEV * RECV_TILE), F32),
            pltpu.VMEM((128, 128), F32),
            pltpu.VMEM((128, 128), F32),
            pltpu.SemaphoreType.DMA((CUTS,)),
            pltpu.SemaphoreType.DMA((CUTS,)),
        ],
        compiler_params=pltpu.CompilerParams(vmem_limit_bytes=60 * 2**20),
        name="buildings",
    )(small, addr_building[0].T, exposure)
    return level.reshape(-1), building.reshape(-1), exposure.T


def solution(mesh):
    both = ("region", "band")
    in_specs = (P(both, None), P(both, None, None), P(both, None), P(both, None, None), P(both, None, None), P(), P(both), P(both, None, None), P(both, None, None))
    out_specs = (P(both), P(both), P(both, None))
    return jax.shard_map(local, mesh=mesh, in_specs=in_specs, out_specs=out_specs, check_vma=False)
```
